256 devices in a mesh: row: 16 (over z, x_hi), col: 16 (over y, x_lo, core).
Axes of the slice: x: 4 (x_hi: 2, x_lo: 2; x = x_hi * 2 + x_lo), y: 4, z: 8, core: 2. Of those that a mesh axis runs over, the one named last changes fastest.
Arguments:
- image_features: bfloat16 [8192, 1152], P(('row', 'col')), may hold values from -6 to 6
- text_features: bfloat16 [8192, 1152], P(('col', 'row')), may hold values from -6 to 6
- image_weight: bfloat16 [1152, 1152], replicated, may hold values from -0.1875 to 0.1875
- text_weight: bfloat16 [1152, 1152], replicated, may hold values from -0.1875 to 0.1875
- log_scale: float32 [1], replicated, may hold values from 2.3 to 3.4
- bias: float32 [1], replicated, may hold values from -4 to -2
Outputs:
- image_grad: float32 [8192, 1152], P(('row', 'col'))
- text_grad: float32 [8192, 1152], P(('col', 'row'))
- image_weight_grad: float32 [1152, 1152], P('row')
- text_weight_grad: float32 [1152, 1152], P('row')
The draws below stay inside these ranges and needn't reach their ends.
All inputs are finite; a program needn't handle non-finite values.
Results may differ from the reference program's by a relative error of at most 0.025.
Values may be sent and summed in bfloat16 or wider, within the bound.
A program may use at most 128 MiB of HBM per device.

```python
import jax
import jax.numpy as jnp
from jax import lax

D = 1152
E = 1152
BATCH = 8192
BLOCK_IMG = 512


def shard_levels(rng, dims, split, least, high):
    def one(position, blocks):
        heights = jax.random.uniform(jax.random.fold_in(jax.random.fold_in(rng, 6), position), (blocks,), jnp.float32, least / len(split), high / len(split))
        return jnp.repeat(jnp.exp(heights), dims[position] // blocks).reshape((-1,) + (1,) * (len(dims) - position - 1))

    loudness = one(*split[0])
    for cut in split[1:]:
        loudness = loudness * one(*cut)
    return loudness


def centred(own_key, dims, scale, limit, split=(), kind=jnp.bfloat16):
    array = jax.random.normal(own_key, dims, jnp.float32) * scale
    if len(split) > 0:
        array = shard_levels(own_key, dims, split, -0.22, 0.18) * array
    return jnp.clip(array, min=-limit, max=limit).astype(kind)


def setup_inputs(seed: int = 0) -> dict:
    keys = jax.random.split(jax.random.key(seed), 7)
    return {
        "image_features": centred(keys[0], (BATCH, D), 1.0, 6.0, ((0, 256),)),
        "text_features": centred(keys[1], (BATCH, D), 1.0, 6.0, ((0, 256),)),
        "image_weight": centred(keys[2], (D, E), D ** -0.5, 0.1875),
        "text_weight": centred(keys[3], (D, E), D ** -0.5, 0.1875),
        "log_scale": jnp.clip(jax.random.uniform(keys[4], (1,), jnp.float32, 2.3, 3.4), 2.3, 3.4),
        "bias": jnp.clip(jax.random.uniform(keys[5], (1,), jnp.float32, -4.0, -2.0), -4.0, -2.0),
    }


def embed_rows(features, weight):
    projected = jnp.dot(features, weight, preferred_element_type=jnp.float32)
    length = jnp.sqrt(lax.optimization_barrier(jnp.sum(projected * projected, axis=1, keepdims=True)) + 1e-06)
    return (length, projected / length)

def unembed_rows(grad_unit, direction, length, features, weight):
    grad_projected = (grad_unit - direction * lax.optimization_barrier(jnp.sum(direction * grad_unit, axis=1, keepdims=True))) / length
    grad_half = grad_projected.astype(jnp.bfloat16)
    grad_features = lax.dot_general(grad_half, weight, (((1,), (1,)), ((), ())), preferred_element_type=jnp.float32)
    grad_weight = lax.dot_general(features, grad_half, (((0,), (0,)), ((), ())), preferred_element_type=jnp.float32)
    return (grad_features, grad_weight)

def pair_weights(image_half, text_half, image_start, text_start, log_scale, bias):
    scores = lax.dot_general(image_half, text_half, (((1,), (1,)), ((), ())), preferred_element_type=jnp.float32)
    factor = jnp.exp(log_scale[0])
    logits = factor * scores + bias[0]
    image_index = image_start + lax.broadcasted_iota(jnp.int32, scores.shape, 0)
    text_index = text_start + lax.broadcasted_iota(jnp.int32, scores.shape, 1)
    labels = jnp.where(image_index == text_index, 1.0, -1.0).astype(jnp.float32)
    return (factor * (-labels * jax.nn.sigmoid(-labels * logits))).astype(jnp.bfloat16)

def reference(image_features, text_features, image_weight, text_weight, log_scale, bias):
    image_length, image_dir = embed_rows(image_features, image_weight)
    text_length, text_dir = embed_rows(text_features, text_weight)
    image_half = image_dir.astype(jnp.bfloat16)
    text_half = text_dir.astype(jnp.bfloat16)
    blocks = image_half.reshape(BATCH // BLOCK_IMG, BLOCK_IMG, E)
    offsets = (jnp.arange(BATCH // BLOCK_IMG) * BLOCK_IMG).astype(jnp.int32)

    def visit(carried, inputs):
        block, offset = inputs
        weights = pair_weights(block, text_half, offset, jnp.int32(0), log_scale, bias)
        grad_block = jnp.dot(weights, text_half, preferred_element_type=jnp.float32)
        carried = carried + lax.dot_general(weights, block, (((0,), (0,)), ((), ())), preferred_element_type=jnp.float32)
        return (carried, grad_block)
    text_grad_dir, image_grad_blocks = lax.scan(visit, jnp.zeros((BATCH, E), jnp.float32), (blocks, offsets))
    image_grad_dir = image_grad_blocks.reshape(BATCH, E)
    image_grad, image_weight_grad = unembed_rows(image_grad_dir, image_dir, image_length, image_features, image_weight)
    text_grad, text_weight_grad = unembed_rows(text_grad_dir, text_dir, text_length, text_features, text_weight)
    return (image_grad, text_grad, image_weight_grad, text_weight_grad)
```

```python
import functools

import jax
import jax.numpy as jnp
from jax import lax
from jax.experimental import pallas as pl
from jax.experimental.pallas import tpu as pltpu
from jax.sharding import PartitionSpec as P

MESH = pl.DeviceIdType.MESH
BF = jnp.bfloat16
F32 = jnp.float32
W = 1152
R = 32
B = 512
Q = 128
U = 72
UP = 80
NB = 9


def place():
    r, c = lax.axis_index("row"), lax.axis_index("col")
    return r // 2, c // 4, (r % 2) * 2 + (c % 4) // 2, c % 2


def device(z, y, x, k):
    return (z * 2 + x // 2, y * 4 + (x % 2) * 2 + k)


def push(src, dst, send, recv, to):
    return pltpu.make_async_remote_copy(
        src_ref=src, dst_ref=dst, send_sem=send, recv_sem=recv, device_id=to, device_id_type=MESH
    )


def dot(a, b):
    return jnp.dot(a, b, preferred_element_type=F32)


def dot_nt(a, b):
    return lax.dot_general(a, b, (((1,), (1,)), ((), ())), preferred_element_type=F32)


def dot_tn(a, b):
    return lax.dot_general(a, b, (((0,), (0,)), ((), ())), preferred_element_type=F32)


def each(lo, hi, fn):
    def step(i, carry):
        fn(i)
        return carry

    lax.fori_loop(lo, hi, step, 0)


def kernel(
    xi, xt, wi_hbm, wt_hbm, ls, bs,
    oi, ot, owi, owt,
    WI, WT, XI, XT, HI, HT, PW, XIT, XTT,
    DI, LI, DT, LT,
    ST, CT, GT, S2, RT, SI, RI, GI,
    GB, PI, TB, PT, PARI, PART, SB, CB, UB, UI, VB, UT, CO, FB,
    wsem, ai_s, ai_r, at_s, at_r, ac_s, ac_r, ct_s, ct_r, rt_s, rt_r, ri_s, ri_r,
    pi_s, pi_r, pt_s, pt_r, cb_s, cb_r, ui_s, ui_r, ut_s, ut_r, fb_s, fb_r,
):
    z, y, x, k = place()
    p0 = y * 4 + x
    sib = device(z, y, x, 1 - k)

    def plane_to(i):
        return device(z, (y + i // 4) % 4, (x + i % 4) % 4, k)

    def plane_back(i):
        return device(z, (y + 4 - i // 4) % 4, (x + 4 - i % 4) % 4, k)

    def line_to(d):
        return device((z + d) % 8, y, x, k)

    def line_back(d):
        return device((z + 8 - d) % 8, y, x, k)

    load_i = pltpu.make_async_copy(wi_hbm, WI, wsem.at[0])
    load_t = pltpu.make_async_copy(wt_hbm, WT, wsem.at[1])
    load_i.start()
    load_t.start()

    bar = pltpu.get_barrier_semaphore()
    each(1, 16, lambda i: pl.semaphore_signal(bar, inc=1, device_id=plane_to(i), device_id_type=MESH))
    each(1, 8, lambda d: pl.semaphore_signal(bar, inc=1, device_id=line_to(d), device_id_type=MESH))
    pl.semaphore_signal(bar, inc=1, device_id=sib, device_id_type=MESH)
    pl.semaphore_wait(bar, 23)

    def ai(i):
        return push(xi, XI.at[i], ai_s.at[i], ai_r.at[i], plane_to(i))

    def at(d):
        return push(xt, XT.at[d], at_s.at[d], at_r.at[d], line_to(d))

    def ac(d):
        return push(XT.at[d], XT.at[8 + d], ac_s.at[d], ac_r.at[d], sib)

    XT[0] = xt[...]
    XI[0] = xi[...]
    each(1, 8, lambda d: at(d).start())
    each(1, 16, lambda i: ai(i).start())
    ac(0).start()

    def forward(d):
        at(d).wait_recv()
        ac(d).start()

    def project(c, X, WW, H, D, L):
        p = dot(X[pl.ds(c * 4, 4)].reshape(Q, W), WW[...])
        length = jnp.sqrt(jnp.sum(p * p, axis=1, keepdims=True) + 1e-06)
        p = p / length
        H[pl.ds(pl.multiple_of(c * Q, Q), Q)] = p.astype(BF)

        @pl.when(c == 0)
        def _():
            D[...] = p[:R]
            L[...] = length[:R]

    forward(1)
    forward(7)
    forward(2)
    forward(6)
    load_i.wait()

    def image_chunk(c):
        def arrive(i):
            @pl.when(i > 0)
            def _():
                ai(i).wait_recv()

        each(c * 4, c * 4 + 4, arrive)
        project(c, XI, WI, HI, DI, LI)

    each(0, 2, image_chunk)
    forward(3)
    forward(5)
    each(2, 4, image_chunk)
    forward(4)
    load_t.wait()

    def text_chunk(c):
        def arrive(s):
            @pl.when(s >= 8)
            def _():
                ac(s - 8).wait_recv()

        each(c * 4, c * 4 + 4, arrive)
        project(c, XT, WT, HT, DT, LT)

    each(0, 4, text_chunk)

    factor = jnp.exp(ls[...])
    bias = bs[...]
    col = lax.broadcasted_iota(jnp.int32, (1, B), 1)
    cs = col >> 5
    cz = (z - (cs & 7)) & 7
    ck = k ^ (cs >> 3)
    tid = (y * 4 + (x % 2) * 2 + ck) * B + (cz * 2 + x // 2) * R + (col & 31)

    def pair_chunk(c):
        row = lax.broadcasted_iota(jnp.int32, (Q, 1), 0) + c * Q
        rs = row >> 5
        ry = (y - (rs >> 2)) & 3
        rx = (x - (rs & 3)) & 3
        iid = (z * 2 + (rx >> 1)) * B + (ry * 4 + ((rx & 1) << 1) + k) * R + (row & 31)
        rows = pl.ds(pl.multiple_of(c * Q, Q), Q)
        logits = factor * dot_nt(HI[rows], HT[...]) + bias
        same = iid == tid
        signed = jnp.where(same, -logits, logits)
        weight = factor / (1.0 + jnp.exp(-signed))
        PW[rows] = jnp.where(same, -weight, weight).astype(BF)

    each(0, 4, pair_chunk)

    def ct(c):
        half = pl.ds(c * 4, 4)
        return push(ST.at[half], CT.at[half], ct_s.at[c], ct_r.at[c], sib)

    def text_grad(c):
        g = dot_tn(PW[:, pl.ds(pl.multiple_of(c * Q, Q), Q)], HI[...])

        @pl.when(c >= 2)
        def _():
            ST[pl.ds((c - 2) * 4, 4)] = g.astype(BF).reshape(4, R, W)
            ct(c - 2).start()

        @pl.when(c < 2)
        def _():
            GT[pl.ds(c * 4, 4)] = g.reshape(4, R, W)

    each(2, 4, text_grad)
    each(0, 2, text_grad)

    def rt(d):
        return push(S2.at[d], RT.at[d], rt_s.at[d], rt_r.at[d], line_back(d))

    def text_send(d):
        @pl.when(d % 4 == 0)
        def _():
            ct(d // 4).wait_recv()

        @pl.when(d > 0)
        def _():
            S2[d] = (GT[d] + CT[d].astype(F32)).astype(BF)
            rt(d).start()

    each(0, 8, text_send)

    def ri(i):
        return push(SI.at[i], RI.at[i], ri_s.at[i], ri_r.at[i], plane_back(i))

    def image_grad(c):
        g = dot(PW[pl.ds(pl.multiple_of(c * Q, Q), Q)], HT[...])
        SI[pl.ds(c * 4, 4)] = g.astype(BF).reshape(4, R, W)

        @pl.when(c == 0)
        def _():
            GI[...] = g[:R]

        def send(i):
            @pl.when(i > 0)
            def _():
                ri(i).start()

        each(c * 4, c * 4 + 4, send)

    each(0, 4, image_grad)

    def flip(j):
        lanes = pl.ds(pl.multiple_of(j * Q, Q), Q)
        XIT[lanes] = XI[:, :, lanes].reshape(B, Q).T
        XTT[lanes] = XT[:, :, lanes].reshape(B, Q).T

    each(0, NB, flip)

    def unembed(g, D, L, blocks):
        d = D[...]
        half = ((g - d * jnp.sum(d * g, axis=1, keepdims=True)) / L[...]).astype(BF)
        for j in range(NB):
            blocks[j] = half[:, j * Q : (j + 1) * Q]
        return half

    def image_sum(i, acc):
        ri(i).wait_recv()
        return acc + RI[i].astype(F32)

    half_i = unembed(lax.fori_loop(1, 16, image_sum, GI[...]), DI, LI, GB)

    def plane_index(i):
        return ((y + i // 4) % 4) * 4 + (x + i % 4) % 4

    def pi(i):
        return push(GB.at[plane_index(i)], PI.at[i], pi_s.at[i], pi_r.at[i], plane_to(i))

    def pi_send(i):
        @pl.when(plane_index(i) < NB)
        def _():
            pi(i).start()

    each(1, 16, pi_send)
    active = p0 < NB

    oi[...] = dot_nt(half_i, WI[...])

    def cb():
        return push(SB, CB, cb_s.at[0], cb_r.at[0], sib)

    def ui(d):
        return push(UB.at[d], UI.at[d], ui_s.at[d], ui_r.at[d], line_to(d))

    def head_rows(zz, h):
        return pl.ds(pl.multiple_of(zz * (2 * U) + h * U, 8), U)

    @pl.when(active)
    def _():
        PI[0] = GB[p0]

        def arrive(i):
            push(GB.at[0], PI.at[i], pi_s.at[i], pi_r.at[i], plane_to(i)).wait_recv()

        each(1, 16, arrive)
        PARI[...] = dot(XIT[...], PI[...].reshape(B, Q))

        def give(d):
            SB[d, 0:U] = PARI[head_rows((z + d) % 8, 1 - k)].astype(BF)
            SB[d, U:UP] = jnp.zeros((UP - U, Q), BF)

        each(0, 8, give)
        cb().start()
        cb().wait_recv()

        def pass_on(d):
            UB[d, 0:U] = (PARI[head_rows((z + d) % 8, k)] + CB[d, 0:U].astype(F32)).astype(BF)
            UB[d, U:UP] = jnp.zeros((UP - U, Q), BF)

            @pl.when(d > 0)
            def _():
                ui(d).start()

        each(0, 8, pass_on)

    def text_sum(d, acc):
        rt(d).wait_recv()
        return acc + RT[d].astype(F32)

    half_t = unembed(lax.fori_loop(1, 8, text_sum, GT[0] + CT[0].astype(F32)), DT, LT, TB)

    def pt(s):
        zz = (z + s % 8) % 8
        kk = (k + s // 8) % 2
        block = jnp.where(kk == 0, zz, 8)
        return push(TB.at[block], PT.at[s], pt_s.at[s], pt_r.at[s], device(zz, y, x, kk))

    each(1, 16, lambda s: pt(s).start())
    PT[0] = TB[jnp.where(k == 0, z, 8)]
    ot[...] = dot_nt(half_t, WT[...])
    each(1, 16, lambda s: pt(s).wait_recv())
    PART[...] = dot(XTT[...], PT[...].reshape(B, Q))

    mine = jnp.where(k == 0, z, 8)

    def ut(u):
        to = device(u // 2, mine // 4, mine % 4, u % 2)
        return push(VB.at[u], UT.at[p0], ut_s.at[u], ut_r.at[p0], to)

    def ut_here(u):
        return (u // 2 == z) & (mine == p0) & (u % 2 == k)

    def ut_used(u):
        return (k == 0) | (u // 2 == z)

    def ut_send(u):
        @pl.when(ut_used(u))
        def _():
            VB[u, 0:U] = PART[pl.ds(pl.multiple_of(u * U, 8), U)].astype(BF)
            VB[u, U:UP] = jnp.zeros((UP - U, Q), BF)

            @pl.when(ut_here(u))
            def _():
                UT[p0] = VB[u]

            @pl.when(jnp.logical_not(ut_here(u)))
            def _():
                ut(u).start()

    each(0, 16, ut_send)

    def fb(t):
        to = device(z, t // 4, k * 2 + (t // 2) % 2, t % 2)
        return push(CO, FB.at[p0], fb_s.at[t], fb_r.at[p0], to)

    def fb_here(t):
        return (t // 4 == y) & (k * 2 + (t // 2) % 2 == x) & (t % 2 == k)

    @pl.when(active)
    def _():
        def add_image(d, acc):
            ui(d).wait_recv()
            return acc + UI[d, 0:U].astype(F32)

        image = lax.fori_loop(1, 8, add_image, UB[0, 0:U].astype(F32))
        own = jnp.where(p0 < 8, (z == p0) & (k == 0), k == 1)

        def add_text(q, acc):
            @pl.when(jnp.logical_not(own & (q == p0)))
            def _():
                push(VB.at[0], UT.at[q], ut_s.at[0], ut_r.at[q], sib).wait_recv()

            return acc + UT[q, 0:U].astype(F32)

        text = lax.fori_loop(0, 16, add_text, jnp.zeros((U, Q), F32))
        CO[...] = jnp.concatenate([image, text], axis=0).astype(BF)

        def send(t):
            @pl.when(fb_here(t))
            def _():
                FB[p0] = CO[...]

            @pl.when(jnp.logical_not(fb_here(t)))
            def _():
                fb(t).start()

        each(0, 16, send)

    for j in range(NB):

        @pl.when(jnp.logical_not((p0 == j) & (x // 2 == k)))
        def _():
            push(CO, FB.at[j], fb_s.at[0], fb_r.at[j], sib).wait_recv()

        both = FB[j].astype(F32)
        owi[:, j * Q : (j + 1) * Q] = both[:U]
        owt[:, j * Q : (j + 1) * Q] = both[U:]

    each(1, 16, lambda i: ai(i).wait_send())
    each(1, 8, lambda d: at(d).wait_send())
    each(0, 8, lambda d: ac(d).wait_send())
    each(0, 2, lambda c: ct(c).wait_send())
    each(1, 8, lambda d: rt(d).wait_send())
    each(1, 16, lambda i: ri(i).wait_send())

    def pi_sent(i):
        @pl.when(plane_index(i) < NB)
        def _():
            pi(i).wait_send()

    each(1, 16, pi_sent)
    each(1, 16, lambda s: pt(s).wait_send())

    def ut_sent(u):
        @pl.when(ut_used(u) & jnp.logical_not(ut_here(u)))
        def _():
            ut(u).wait_send()

    each(0, 16, ut_sent)

    @pl.when(active)
    def _():
        cb().wait_send()
        each(1, 8, lambda d: ui(d).wait_send())

        def fb_sent(t):
            @pl.when(jnp.logical_not(fb_here(t)))
            def _():
                fb(t).wait_send()

        each(0, 16, fb_sent)


def body(image_features, text_features, image_weight, text_weight, log_scale, bias):
    vmem = pl.BlockSpec(memory_space=pltpu.VMEM)
    hbm = pl.BlockSpec(memory_space=pl.ANY)
    v = pltpu.VMEM
    dma = pltpu.SemaphoreType.DMA
    return pl.pallas_call(
        kernel,
        out_shape=(
            jax.ShapeDtypeStruct((R, W), F32),
            jax.ShapeDtypeStruct((R, W), F32),
            jax.ShapeDtypeStruct((U, W), F32),
            jax.ShapeDtypeStruct((U, W), F32),
        ),
        in_specs=[vmem, vmem, hbm, hbm, vmem, vmem],
        out_specs=(vmem, vmem, vmem, vmem),
        scratch_shapes=[
            v((W, W), BF), v((W, W), BF), v((16, R, W), BF), v((16, R, W), BF), v((B, W), BF), v((B, W), BF), v((B, B), BF),
            v((W, B), BF), v((W, B), BF),
            v((R, W), F32), v((R, 1), F32), v((R, W), F32), v((R, 1), F32),
            v((8, R, W), BF), v((8, R, W), BF), v((8, R, W), F32), v((8, R, W), BF), v((8, R, W), BF),
            v((16, R, W), BF), v((16, R, W), BF), v((R, W), F32),
            v((NB, R, Q), BF), v((16, R, Q), BF), v((NB, R, Q), BF), v((16, R, Q), BF), v((W, Q), F32), v((W, Q), F32),
            v((8, UP, Q), BF), v((8, UP, Q), BF), v((8, UP, Q), BF), v((8, UP, Q), BF), v((16, UP, Q), BF), v((16, UP, Q), BF),
            v((2 * U, Q), BF), v((NB, 2 * U, Q), BF),
            dma((2,)), dma((16,)), dma((16,)), dma((8,)), dma((8,)), dma((8,)), dma((8,)), dma((2,)), dma((2,)), dma((8,)), dma((8,)),
            dma((16,)), dma((16,)), dma((16,)), dma((16,)), dma((16,)), dma((16,)), dma((1,)), dma((1,)), dma((8,)), dma((8,)),
            dma((16,)), dma((16,)), dma((16,)), dma((NB,)),
        ],
        compiler_params=pltpu.CompilerParams(
            collective_id=0, has_side_effects=True, vmem_limit_bytes=50 * 1024 * 1024
        ),
    )(
        image_features, text_features, image_weight, text_weight,
        log_scale.reshape(1, 1), bias.reshape(1, 1),
    )


def solution(mesh):
    in_specs = (P(("row", "col"), None), P(("col", "row"), None), P(), P(), P(), P())
    out_specs = (P(("row", "col"), None), P(("col", "row"), None), P("row", None), P("row", None))
    return jax.shard_map(body, mesh=mesh, in_specs=in_specs, out_specs=out_specs, check_vma=False)
```

```python
import jax
import jax.numpy as jnp
from jax import lax
from jax.experimental import pallas as pl
from jax.experimental.pallas import tpu as pltpu
from jax.sharding import PartitionSpec as P

MESH = pl.DeviceIdType.MESH
BF = jnp.bfloat16
F32 = jnp.float32
W = 1152
R = 32
H = 16
B = 512
Q = 128
U = 72
UP = 80
NB = 9
TEXT_AT = 7
ORDER = (0, 1, 7, 2, 6, 3, 5, 4)
POS = {d: n for n, d in enumerate(ORDER)}


def place():
    r, c = lax.axis_index("row"), lax.axis_index("col")
    return r // 2, c // 4, (r % 2) * 2 + (c % 4) // 2, c % 2


def other(s):
    return 8 + (s + 4) % 8


def device(z, y, x, k):
    return (z * 2 + x // 2, y * 4 + (x % 2) * 2 + k)


def push(src, dst, send, recv, to):
    return pltpu.make_async_remote_copy(
        src_ref=src, dst_ref=dst, send_sem=send, recv_sem=recv, device_id=to, device_id_type=MESH
    )


def dot(a, b):
    return jnp.dot(a, b, preferred_element_type=F32)


def dot_nt(a, b):
    return lax.dot_general(a, b, (((1,), (1,)), ((), ())), preferred_element_type=F32)


def dot_tn(a, b):
    return lax.dot_general(a, b, (((0,), (0,)), ((), ())), preferred_element_type=F32)


def each(lo, hi, fn):
    def step(i, carry):
        fn(i)
        return carry

    lax.fori_loop(lo, hi, step, 0)


def kernel(
    both_x, wi_hbm, wt_hbm, ls, bs,
    out,
    WI, WT, XI, XT, HI, HT, PW, XIT, XTT,
    DI, LI, DT, LT,
    ST, CT, GT, S2, RA, RB, RM, RT, SI, R1, R2, N1, N2, F1, F2,
    GB, PI, TB, PT, PARI, PART, SB, CB, UB, UI, VB, UT, CI, CX, FI, FT,
    lsem, at_s, at_r, ac_s, ac_r, ax_s, ax_r, ay_s, ay_r, a1_s, a1_r, a2_s, a2_r,
    ct_s, ct_r, ra_s, ra_r, rb_s, rb_r, rt_s, rt_r, r1_s, r1_r, r2_s, r2_r, f1_s, f1_r, f2_s, f2_r,
    pi_s, pi_r, pt_s, pt_r, cb_s, cb_r, ui_s, ui_r, ut_s, ut_r, fi_s, fi_r, ft_s, ft_r,
):
    z, y, x, k = place()
    p0 = y * 4 + x
    sib = device(z, y, x, 1 - k)

    def at_z(d):
        return device((z + d + 8) % 8, y, x, k)

    def at_y(d):
        return device(z, (y + d + 4) % 4, x, k)

    def at_x(d):
        return device(z, y, (x + d + 4) % 4, k)

    loads = [
        pltpu.make_async_copy(src, dst, lsem.at[n])
        for n, (src, dst) in enumerate(((both_x.at[1], XT.at[0]), (both_x.at[0], XI.at[0, 0]), (wt_hbm, WT), (wi_hbm, WI)))
    ]
    for load in loads:
        load.start()

    bar = pltpu.get_barrier_semaphore()
    near = [at_z(d) for d in (1, -1, 2, -2)] + [at_x(d) for d in (1, 2, 3)] + [at_y(d) for d in (1, 2, 3)] + [sib]
    for to in near:
        pl.semaphore_signal(bar, inc=1, device_id=to, device_id_type=MESH)

    pad = jnp.zeros((8, UP - U, Q), BF)
    for buf in (SB, UB, VB.at[0:8], VB.at[8:16]):
        buf[:, U:UP] = pad
    CI[U:UP] = pad[0]
    CX[U:UP] = pad[0]

    loads[0].wait()
    loads[1].wait()
    pl.semaphore_wait(bar, len(near))

    def tz(d, d_to, n, rows=None):
        src, dst = XT.at[POS[d % 8]], XT.at[POS[(d + d_to) % 8]]
        if rows is not None:
            src, dst = src.at[pl.ds(rows, H)], dst.at[pl.ds(rows, H)]
        return push(src, dst, at_s.at[n], at_r.at[n], at_z(d_to))

    z_near = {1: tz(0, 1, 0), 7: tz(0, -1, 1), 2: tz(0, 2, 2), 6: tz(0, -2, 3)}
    z_far = {3: tz(2, 1, 4), 5: tz(-2, -1, 5), 4: tz(2, 2, 6, 0), 12: tz(-2, -2, 7, H)}

    def ac(s):
        return push(XT.at[s], XT.at[other(s)], ac_s.at[s], ac_r.at[s], sib)

    def ax(d):
        return push(XI.at[0, 0], XI.at[0, d], ax_s.at[d], ax_r.at[d], at_x(d))

    def ay(d):
        return push(XI.at[0, 0], XI.at[d, 0], ay_s.at[d], ay_r.at[d], at_y(d))

    def a1(d):
        rows = pl.ds(0, H)
        return push(XI.at[0, 1:4, rows], XI.at[d, 1:4, rows], a1_s.at[d], a1_r.at[d], at_y(d))

    def a2(d):
        rows = pl.ds(H, H)
        return push(XI.at[1:4, 0, rows], XI.at[1:4, d, rows], a2_s.at[d], a2_r.at[d], at_x(d))

    z_near[2].start()
    z_near[6].start()
    for d in (2, 1, 3):
        ax(d).start()
        ay(d).start()
    z_near[1].start()
    z_near[7].start()
    ac(0).start()

    def project(x_in, n, WW, HH, c):
        p = dot(x_in.reshape(n * Q, W), WW[...])
        length = jnp.sqrt(jnp.sum(p * p, axis=1, keepdims=True) + 1e-06)
        p = p * (1.0 / length)
        HH[c * Q : (c + n) * Q] = p.astype(BF)
        return p, length

    def arrived(copies):
        for copy in copies:
            copy.wait_recv()

    def relay():
        z_near[2].wait_recv()
        z_far[4].start()
        z_far[3].start()
        ac(POS[2]).start()
        z_near[6].wait_recv()
        z_far[12].start()
        z_far[5].start()
        ac(POS[6]).start()
        for d in (1, 7):
            z_near[d].wait_recv()
            ac(POS[d]).start()

    relay()
    arrived(ax(d) for d in (1, 3, 2))
    for d in (2, 1, 3):
        a1(d).start()
    arrived(ay(d) for d in (1, 3, 2))
    for d in (2, 1, 3):
        a2(d).start()

    loads[2].wait()
    p, length = project(XT[0:4], 1, WT, HT, 0)
    DT[...] = p[:R]
    LT[...] = length[:R]
    loads[3].wait()
    p, length = project(XI[0], 1, WI, HI, 0)
    DI[...] = p[:R]
    LI[...] = length[:R]

    arrived([z_far[3]])
    ac(POS[3]).start()
    arrived([z_far[5]])
    ac(POS[5]).start()
    arrived([z_far[4], z_far[12]])
    ac(POS[4]).start()
    arrived(ac(s) for s in range(4))
    project(XT[12:16], 1, WT, HT, 3)
    arrived(a2(d) for d in (1, 2, 3))
    arrived(a1(d) for d in (1, 3, 2))
    project(XI[1:4], 3, WI, HI, 1)
    arrived(ac(s) for s in range(4, 8))
    project(XT[4:12], 2, WT, HT, 1)

    factor = jnp.exp(ls[...])
    bias = bs[...]
    col = lax.broadcasted_iota(jnp.int32, (1, B), 1)
    cs = col >> 5
    cd = jnp.zeros_like(cs)
    for n, d in enumerate(ORDER):
        cd = jnp.where((cs == n) | (cs == other(n)), d, cd)
    cz = (z - cd) & 7
    ck = k ^ (cs >> 3)
    tid = (y * 4 + (x % 2) * 2 + ck) * B + (cz * 2 + x // 2) * R + (col & 31)
    row = lax.broadcasted_iota(jnp.int32, (B, 1), 0)
    rs = row >> 5
    ry = (y - (rs >> 2)) & 3
    rx = (x - (rs & 3)) & 3
    iid = (z * 2 + (rx >> 1)) * B + (ry * 4 + ((rx & 1) << 1) + k) * R + (row & 31)

    def pair(c, n):
        cols = slice(c * Q, (c + n) * Q)
        logits = factor * dot_nt(HI[...], HT[cols]) + bias
        same = iid == tid[:, cols]
        signed = jnp.where(same, -logits, logits)
        weight = factor / (1.0 + jnp.exp(-signed))
        PW[:, cols] = jnp.where(same, -weight, weight).astype(BF)

    def text_grad(c):
        return dot_tn(PW[:, c * Q : (c + 1) * Q], HI[...]).reshape(4, R, W)

    def ct(c):
        half = pl.ds(c * 4, 4)
        return push(ST.at[half], CT.at[half], ct_s.at[c], ct_r.at[c], sib)

    near_t = {1: push(S2.at[0], RT.at[0], rt_s.at[0], rt_r.at[0], at_z(-1)),
              7: push(S2.at[1], RT.at[1], rt_s.at[1], rt_r.at[1], at_z(1))}
    relay_t = {3: push(S2.at[2], RA.at[0], ra_s.at[0], ra_r.at[0], at_z(-1)),
               5: push(S2.at[3], RA.at[1], ra_s.at[1], ra_r.at[1], at_z(1))}
    half_t = [push(S2.at[4, pl.ds(n * H, H)], RB.at[n], rb_s.at[n], rb_r.at[n], at_z(2 * (2 * n - 1))) for n in (0, 1)]
    sum_t = [push(RM.at[n], RT.at[2 + n], rt_s.at[2 + n], rt_r.at[2 + n], at_z(2 * (2 * n - 1))) for n in (0, 1)]

    def both(d):
        return GT[POS[d]] + CT[POS[d]].astype(F32)

    pair(1, 2)
    ST[4:8] = text_grad(2).astype(BF)
    ct(1).start()
    GT[4:8] = text_grad(1)
    pair(0, 1)
    pair(3, 1)
    ct(1).wait_recv()
    S2[4] = both(4).astype(BF)
    half_t[0].start()
    half_t[1].start()
    S2[2] = both(3).astype(BF)
    relay_t[3].start()
    S2[3] = both(5).astype(BF)
    relay_t[5].start()
    ST[0:4] = text_grad(3).astype(BF)
    ct(0).start()

    def r1(d):
        return push(SI.at[d, :, pl.ds(0, H)], R1.at[d], r1_s.at[d], r1_r.at[d], at_y(-d))

    def r2(d):
        return push(SI.at[:, d, pl.ds(H, H)], R2.at[d], r2_s.at[d], r2_r.at[d], at_x(-d))

    for c in (2, 1, 3, 0):
        SI[c] = dot(PW[c * Q : (c + 1) * Q], HT[...]).astype(BF).reshape(4, R, W)
        if c > 0:
            r1(c).start()
    for d in (2, 1, 3):
        r2(d).start()

    GT[0:4] = text_grad(0)
    ct(0).wait_recv()
    S2[0] = both(1).astype(BF)
    near_t[1].start()
    S2[1] = both(7).astype(BF)
    near_t[7].start()

    for n, (d_near, d_far) in enumerate(((2, 3), (6, 5))):
        relay_t[d_far].wait_recv()
        half_t[n].wait_recv()
        m = both(d_near) + RA[n].astype(F32)
        extra = RB[n].astype(F32)
        rows, rest = (slice(0, H), slice(H, R)) if n == 0 else (slice(H, R), slice(0, H))
        RM[n, rows] = (m[rows] + extra).astype(BF)
        RM[n, rest] = m[rest].astype(BF)
        sum_t[n].start()

    def flip(j):
        lanes = pl.ds(pl.multiple_of(j * Q, Q), Q)
        XIT[lanes] = XI[:, :, :, lanes].reshape(B, Q).T
        XTT[lanes] = XT[:, :, lanes].reshape(B, Q).T

    each(0, NB, flip)

    def f1(d):
        return push(N1.at[d], F1.at[d], f1_s.at[d], f1_r.at[d], at_x(-d))

    def f2(d):
        return push(N2.at[d], F2.at[d], f2_s.at[d], f2_r.at[d], at_y(-d))

    arrived(r1(d) for d in (1, 3, 2))

    def sum1(d):
        N1[d] = (SI[0, d, 0:H].astype(F32) + R1[1, d].astype(F32) + R1[2, d].astype(F32) + R1[3, d].astype(F32)).astype(BF)

    def sum2(d):
        N2[d] = (SI[d, 0, H:R].astype(F32) + R2[1, d].astype(F32) + R2[2, d].astype(F32) + R2[3, d].astype(F32)).astype(BF)

    for d in (2, 1, 3):
        sum1(d)
        f1(d).start()
    sum1(0)
    arrived(r2(d) for d in (1, 3, 2))
    for d in (2, 1, 3):
        sum2(d)
        f2(d).start()
    sum2(0)

    def unembed(g, D, L, blocks):
        d = D[...]
        half = ((g - d * jnp.sum(d * g, axis=1, keepdims=True)) / L[...]).astype(BF)
        for j in range(NB):
            blocks[j] = half[:, j * Q : (j + 1) * Q]
        return half

    arrived((near_t[1], near_t[7], sum_t[0], sum_t[1]))
    g = both(0)
    for n in range(4):
        g = g + RT[n].astype(F32)
    half_text = unembed(g, DT, LT, TB)
    mine = jnp.where(k == 0, z, 8)

    def pt(s):
        zz = (z + s % 8) % 8
        kk = (k + s // 8) % 2
        slot = POS[s % 8] if s < 8 else other(POS[s % 8])
        return push(TB.at[jnp.where(kk == 0, zz, 8)], PT.at[slot], pt_s.at[s], pt_r.at[s], device(zz, y, x, kk))

    for s in range(1, 16):
        pt(s).start()
    PT[0] = TB[mine]

    arrived(f1(d) for d in (1, 3, 2))
    arrived(f2(d) for d in (1, 3, 2))
    g1 = N1[0].astype(F32)
    g2 = N2[0].astype(F32)
    for d in (1, 2, 3):
        g1 = g1 + F1[d].astype(F32)
        g2 = g2 + F2[d].astype(F32)
    half_image = unembed(jnp.concatenate([g1, g2], axis=0), DI, LI, GB)

    def plane_index(i):
        return ((y + i // 4) % 4) * 4 + (x + i % 4) % 4

    def pi(i, block=None):
        block = plane_index(i) if block is None else block
        to = device(z, (y + i // 4) % 4, (x + i % 4) % 4, k)
        return push(GB.at[block], PI.at[i], pi_s.at[i], pi_r.at[i], to)

    def pi_send(i):
        @pl.when(plane_index(i) < NB)
        def _():
            pi(i).start()

    each(1, 16, pi_send)
    sums_image = p0 < NB

    for s in range(1, 16):
        pt(s).wait_recv()
    PART[...] = dot(XTT[...], PT[...].reshape(B, Q))
    sums_text = p0 >= TEXT_AT

    def ut(u):
        at = TEXT_AT + mine
        return push(VB.at[u], UT.at[p0], ut_s.at[u], ut_r.at[p0], device(u // 2, at // 4, at % 4, u % 2))

    def ut_here(u):
        return (u // 2 == z) & (TEXT_AT + mine == p0) & (u % 2 == k)

    def ut_used(u):
        return (k == 0) | (u // 2 == z)

    def ut_send(i):
        u = (i + 2 * z + 8) % 16

        @pl.when(ut_used(u))
        def _():
            VB[u, 0:U] = PART[pl.ds(pl.multiple_of(u * U, 8), U)].astype(BF)

            @pl.when(ut_here(u))
            def _():
                UT[p0] = VB[u]

            @pl.when(jnp.logical_not(ut_here(u)))
            def _():
                ut(u).start()

    each(0, 16, ut_send)

    def cb():
        return push(SB, CB, cb_s.at[0], cb_r.at[0], sib)

    def ui(d):
        return push(UB.at[d], UI.at[d], ui_s.at[d], ui_r.at[d], device((z + d) % 8, y, x, k))

    def head_rows(zz, h):
        return pl.ds(pl.multiple_of(zz * (2 * U) + h * U, 8), U)

    @pl.when(sums_image)
    def _():
        PI[0] = GB[p0]
        each(1, 16, lambda i: pi(i, 0).wait_recv())
        PARI[...] = dot(XIT[...], PI[...].reshape(B, Q))

        def give(d):
            SB[d, 0:U] = PARI[head_rows((z + d) % 8, 1 - k)].astype(BF)

        each(0, 8, give)
        cb().start()

    out[R : 2 * R] = dot_nt(half_text, WT[...])

    @pl.when(sums_image)
    def _():
        cb().wait_recv()

        def pass_on(d):
            UB[d, 0:U] = (PARI[head_rows((z + d) % 8, k)] + CB[d, 0:U].astype(F32)).astype(BF)

            @pl.when(d > 0)
            def _():
                ui(d).start()

        each(0, 8, pass_on)

    def spread(t):
        return device(z, (y + 2 + t // 4) % 4, k * 2 + (t // 2) % 2, t % 2)

    def here(t):
        return (t // 4 == 2) & (k * 2 + (t // 2) % 2 == x) & (t % 2 == k)

    def fi(t):
        return push(CI, FI.at[p0], fi_s.at[t], fi_r.at[p0], spread(t))

    def ft(t):
        return push(CX, FT.at[p0 - TEXT_AT], ft_s.at[t], ft_r.at[p0 - TEXT_AT], spread(t))

    out[0:R] = dot_nt(half_image, WI[...])

    @pl.when(sums_image)
    def _():
        def add_image(d, acc):
            ui(d).wait_recv()
            return acc + UI[d, 0:U].astype(F32)

        CI[0:U] = lax.fori_loop(1, 8, add_image, UB[0, 0:U].astype(F32)).astype(BF)

        def send(t):
            @pl.when(here(t))
            def _():
                FI[p0] = CI[...]

            @pl.when(jnp.logical_not(here(t)))
            def _():
                fi(t).start()

        each(0, 16, send)

    @pl.when(sums_text)
    def _():
        block = p0 - TEXT_AT
        own = jnp.where(block < 8, (z == block) & (k == 0), k == 1)

        def add_text(q, acc):
            @pl.when(jnp.logical_not(own & (q == p0)))
            def _():
                push(VB.at[0], UT.at[q], ut_s.at[0], ut_r.at[q], sib).wait_recv()

            return acc + UT[q, 0:U].astype(F32)

        CX[0:U] = lax.fori_loop(0, 16, add_text, jnp.zeros((U, Q), F32)).astype(BF)

        def send(t):
            @pl.when(here(t))
            def _():
                FT[block] = CX[...]

            @pl.when(jnp.logical_not(here(t)))
            def _():
                ft(t).start()

        each(0, 16, send)

    for j in range(NB):
        lanes = slice(j * Q, (j + 1) * Q)

        @pl.when(jnp.logical_not((p0 == j) & (x // 2 == k)))
        def _():
            push(CI, FI.at[j], fi_s.at[0], fi_r.at[j], sib).wait_recv()

        out[2 * R : 2 * R + U, lanes] = FI[j, 0:U].astype(F32)

    for j in range(NB):
        lanes = slice(j * Q, (j + 1) * Q)

        @pl.when(jnp.logical_not((p0 == j + TEXT_AT) & (x // 2 == k)))
        def _():
            push(CX, FT.at[j], ft_s.at[0], ft_r.at[j], sib).wait_recv()

        out[2 * R + U :, lanes] = FT[j, 0:U].astype(F32)

    for copy in (*z_near.values(), *z_far.values(), *near_t.values(), *relay_t.values(), *half_t, *sum_t):
        copy.wait_send()
    each(0, 8, lambda s: ac(s).wait_send())
    for copy in (ax, ay, a1, a2, r1, r2, f1, f2):
        for d in (1, 2, 3):
            copy(d).wait_send()
    ct(0).wait_send()
    ct(1).wait_send()
    for s in range(1, 16):
        pt(s).wait_send()

    def pi_sent(i):
        @pl.when(plane_index(i) < NB)
        def _():
            pi(i).wait_send()

    each(1, 16, pi_sent)

    def ut_sent(u):
        @pl.when(ut_used(u) & jnp.logical_not(ut_here(u)))
        def _():
            ut(u).wait_send()

    each(0, 16, ut_sent)

    @pl.when(sums_image)
    def _():
        cb().wait_send()
        each(1, 8, lambda d: ui(d).wait_send())

        def sent(t):
            @pl.when(jnp.logical_not(here(t)))
            def _():
                fi(t).wait_send()

        each(0, 16, sent)

    @pl.when(sums_text)
    def _():
        def sent(t):
            @pl.when(jnp.logical_not(here(t)))
            def _():
                ft(t).wait_send()

        each(0, 16, sent)


def body(image_features, text_features, image_weight, text_weight, log_scale, bias):
    vmem = pl.BlockSpec(memory_space=pltpu.VMEM)
    hbm = pl.BlockSpec(memory_space=pltpu.HBM)
    v = pltpu.VMEM
    dma = pltpu.SemaphoreType.DMA
    results = pl.pallas_call(
        kernel,
        out_shape=jax.ShapeDtypeStruct((2 * R + 2 * U, W), F32),
        in_specs=[hbm, hbm, hbm, vmem, vmem],
        out_specs=vmem,
        scratch_shapes=[
            v((W, W), BF), v((W, W), BF), v((4, 4, R, W), BF), v((16, R, W), BF), v((B, W), BF), v((B, W), BF), v((B, B), BF),
            v((W, B), BF), v((W, B), BF),
            v((R, W), F32), v((R, 1), F32), v((R, W), F32), v((R, 1), F32),
            v((8, R, W), BF), v((8, R, W), BF), v((8, R, W), F32), v((5, R, W), BF),
            v((2, R, W), BF), v((2, H, W), BF), v((2, R, W), BF), v((4, R, W), BF),
            v((4, 4, R, W), BF), v((4, 4, H, W), BF), v((4, 4, H, W), BF), v((4, H, W), BF), v((4, H, W), BF), v((4, H, W), BF), v((4, H, W), BF),
            v((NB, R, Q), BF), v((16, R, Q), BF), v((NB, R, Q), BF), v((16, R, Q), BF), v((W, Q), F32), v((W, Q), F32),
            v((8, UP, Q), BF), v((8, UP, Q), BF), v((8, UP, Q), BF), v((8, UP, Q), BF), v((16, UP, Q), BF), v((16, UP, Q), BF),
            v((UP, Q), BF), v((UP, Q), BF), v((NB, UP, Q), BF), v((NB, UP, Q), BF),
            dma((4,)), dma((8,)), dma((8,)), dma((8,)), dma((8,)), *[dma((4,)) for _ in range(8)],
            dma((2,)), dma((2,)), dma((2,)), dma((2,)), dma((2,)), dma((2,)), dma((4,)), dma((4,)), *[dma((4,)) for _ in range(8)],
            dma((16,)), dma((16,)), dma((16,)), dma((16,)), dma((1,)), dma((1,)), dma((8,)), dma((8,)),
            dma((16,)), dma((16,)), dma((16,)), dma((NB,)), dma((16,)), dma((NB,)),
        ],
        compiler_params=pltpu.CompilerParams(
            collective_id=0, has_side_effects=True, vmem_limit_bytes=52 * 1024 * 1024
        ),
    )(
        jnp.stack([image_features, text_features]), image_weight, text_weight,
        log_scale.reshape(1, 1), bias.reshape(1, 1),
    )

    return results[:R], results[R : 2 * R], results[2 * R : 2 * R + U], results[2 * R + U :]


def solution(mesh):
    in_specs = (P(("row", "col"), None), P(("col", "row"), None), P(), P(), P(), P())
    out_specs = (P(("row", "col"), None), P(("col", "row"), None), P("row", None), P("row", None))
    return jax.shard_map(body, mesh=mesh, in_specs=in_specs, out_specs=out_specs, check_vma=False)
```

```python
import jax
import jax.numpy as jnp
from jax import lax
from jax.experimental import pallas as pl
from jax.experimental.pallas import tpu as pltpu
from jax.sharding import PartitionSpec as P

MESH = pl.DeviceIdType.MESH
BF = jnp.bfloat16
F32 = jnp.float32
W = 1152
R = 32
H = 16
B = 512
Q = 128
U = 72
UP = 80
NB = 9
POS = {6: 0, 3: 1, 5: 2, 4: 3, 0: 8, 1: 9, 7: 10, 2: 11}
OWN = POS[0]


def div(a, b):
    return a // b if isinstance(a, int) else lax.div(a, jnp.int32(b))


def rem(a, b):
    return a % b if isinstance(a, int) else lax.rem(a, jnp.int32(b))


def place():
    r, c = lax.axis_index("row"), lax.axis_index("col")
    return div(r, 2), div(c, 4), rem(r, 2) * 2 + div(rem(c, 4), 2), rem(c, 2)


def device(z, y, x, k):
    return (z * 2 + div(x, 2), y * 4 + rem(x, 2) * 2 + k)


def push(src, dst, send, recv, to):
    return pltpu.make_async_remote_copy(
        src_ref=src, dst_ref=dst, send_sem=send, recv_sem=recv, device_id=to, device_id_type=MESH
    )


def dot(a, b):
    return jnp.dot(a, b, preferred_element_type=F32)


def dot_nt(a, b):
    return lax.dot_general(a, b, (((1,), (1,)), ((), ())), preferred_element_type=F32)


def dot_tn(a, b):
    return lax.dot_general(a, b, (((0,), (0,)), ((), ())), preferred_element_type=F32)


def each(lo, hi, fn):
    def step(i, carry):
        fn(i)
        return carry

    lax.fori_loop(lo, hi, step, 0)


def kernel(
    both_x, wi_hbm, wt_hbm, ls, bs,
    out,
    WI, WT, XI, XT, HI, HT, PW, XIT, XTT,
    DI, LI, DT, LT,
    ST, CT, GT, S2, RA, RB, RM, RT, SI, R1, R2, N1, N2, F1, F2,
    GB, PI, TB, PT, PARI, PART, SB, CB, UB, UI, VB, UT, CI, CX, FI, FT,
    lsem, at_s, at_r, ac_s, ac_r, ax_s, ax_r, ay_s, ay_r, a1_s, a1_r, a2_s, a2_r,
    ct_s, ct_r, ra_s, ra_r, rb_s, rb_r, rt_s, rt_r, r1_s, r1_r, r2_s, r2_r, e1_s, e1_r, e2_s, e2_r, f1_s, f1_r, f2_s, f2_r,
    pi_s, pi_r, pt_s, pt_r, cb_s, cb_r, ui_s, ui_r, ut_s, ut_r, fi_s, fi_r, ft_s, ft_r,
):
    z, y, x, k = place()
    p0 = y * 4 + x
    sib = device(z, y, x, 1 - k)

    def at_z(d):
        return device(rem(z + d + 8, 8), y, x, k)

    def at_y(d):
        return device(z, rem(y + d + 4, 4), x, k)

    def at_x(d):
        return device(z, y, rem(x + d + 4, 4), k)

    loads = [
        pltpu.make_async_copy(src, dst, lsem.at[n])
        for n, (src, dst) in enumerate(((both_x.at[1], XT.at[OWN]), (both_x.at[0], XI.at[0, 0]), (wt_hbm, WT), (wi_hbm, WI)))
    ]
    for load in loads:
        load.start()

    bar = pltpu.get_barrier_semaphore()
    near = [at_z(d) for d in (1, -1, 2, -2)] + [at_x(d) for d in (1, 2, 3)] + [at_y(d) for d in (1, 2, 3)] + [sib]
    for to in near:
        pl.semaphore_signal(bar, inc=1, device_id=to, device_id_type=MESH)

    pad = jnp.zeros((8, UP - U, Q), BF)
    for buf in (SB, UB, VB.at[0:8], VB.at[8:16]):
        buf[:, U:UP] = pad
    CI[U:UP] = pad[0]
    CX[U:UP] = pad[0]

    loads[0].wait()
    loads[1].wait()
    pl.semaphore_wait(bar, len(near))

    def tz(d, d_to, n, rows=None):
        src, dst = XT.at[POS[d % 8]], XT.at[POS[(d + d_to) % 8]]
        if rows is not None:
            src, dst = src.at[pl.ds(rows, H)], dst.at[pl.ds(rows, H)]
        return push(src, dst, at_s.at[n], at_r.at[n], at_z(d_to))

    z_near = {1: tz(0, 1, 0), 7: tz(0, -1, 1), 2: tz(0, 2, 2), 6: tz(0, -2, 3)}
    z_far = {3: tz(2, 1, 4), 5: tz(-2, -1, 5), 4: tz(2, 2, 6, 0), 12: tz(-2, -2, 7, H)}

    def ac(s):
        return push(XT.at[s], XT.at[s + 4], ac_s.at[s], ac_r.at[s], sib)

    def ax(d):
        return push(XI.at[0, 0], XI.at[0, d], ax_s.at[d], ax_r.at[d], at_x(d))

    def ay(d):
        return push(XI.at[0, 0], XI.at[d, 0], ay_s.at[d], ay_r.at[d], at_y(d))

    def a1(d, e):
        rows = pl.ds(0, H)
        n = 4 * d + e
        return push(XI.at[0, e, rows], XI.at[d, e, rows], a1_s.at[n], a1_r.at[n], at_y(d))

    def a2(d, e):
        rows = pl.ds(H, H)
        n = 4 * d + e
        return push(XI.at[e, 0, rows], XI.at[e, d, rows], a2_s.at[n], a2_r.at[n], at_x(d))

    def relay_x(e):
        ax(e).wait_recv()
        for d in (2, 1, 3):
            a1(d, e).start()

    def relay_y(e):
        ay(e).wait_recv()
        for d in (2, 1, 3):
            a2(d, e).start()

    z_near[2].start()
    z_near[6].start()
    for d in (2, 1, 3):
        ax(d).start()
        ay(d).start()
    z_near[1].start()
    z_near[7].start()
    ac(OWN).start()

    def project(x_in, n, WW, HH, c):
        p = dot(x_in.reshape(n * Q, W), WW[...])
        length = jnp.sqrt(jnp.sum(p * p, axis=1, keepdims=True) + 1e-06)
        p = p * (1.0 / length)
        HH[c * Q : (c + n) * Q] = p.astype(BF)
        return p, length

    def arrived(copies):
        for copy in copies:
            copy.wait_recv()

    for e in (1, 3):
        relay_x(e)
        relay_y(e)
    z_near[2].wait_recv()
    z_far[4].start()
    z_far[3].start()
    ac(POS[2]).start()
    z_near[6].wait_recv()
    z_far[12].start()
    z_far[5].start()
    relay_x(2)
    relay_y(2)
    ac(POS[6]).start()
    for d in (1, 7):
        z_near[d].wait_recv()
        ac(POS[d]).start()

    loads[2].wait()
    p, length = project(XT[8:12], 1, WT, HT, 2)
    DT[...] = p[:R]
    LT[...] = length[:R]
    loads[3].wait()
    p, length = project(XI[0], 1, WI, HI, 0)
    DI[...] = p[:R]
    LI[...] = length[:R]

    arrived([z_far[3]])
    ac(POS[3]).start()
    arrived([z_far[5]])
    ac(POS[5]).start()
    arrived([z_far[4], z_far[12]])
    ac(POS[4]).start()
    arrived(ac(s) for s in (8, 9, 10, 11))
    project(XT[12:16], 1, WT, HT, 3)
    arrived(ac(s) for s in range(4))
    project(XT[0:8], 2, WT, HT, 0)
    arrived(a(d, e) for a in (a1, a2) for d in (1, 3, 2) for e in (1, 3, 2))
    project(XI[1:4], 3, WI, HI, 1)

    factor = jnp.exp(ls[...])
    bias = bs[...]
    col = lax.broadcasted_iota(jnp.int32, (1, B), 1)
    cs = col >> 5
    cd = jnp.zeros_like(cs)
    for d, n in POS.items():
        cd = jnp.where((cs & 11) == n, d, cd)
    cz = (z - cd) & 7
    ck = k ^ ((cs >> 2) & 1)
    tid = (y * 4 + rem(x, 2) * 2 + ck) * B + (cz * 2 + div(x, 2)) * R + (col & 31)
    row = lax.broadcasted_iota(jnp.int32, (B, 1), 0)
    rs = row >> 5
    ry = (y - (rs >> 2)) & 3
    rx = (x - (rs & 3)) & 3
    iid = (z * 2 + (rx >> 1)) * B + (ry * 4 + ((rx & 1) << 1) + k) * R + (row & 31)

    def pair(c, n):
        cols = slice(c * Q, (c + n) * Q)
        logits = factor * dot_nt(HI[...], HT[cols]) + bias
        same = iid == tid[:, cols]
        signed = jnp.where(same, -logits, logits)
        weight = factor / (1.0 + jnp.exp(-signed))
        PW[:, cols] = jnp.where(same, -weight, weight).astype(BF)

    def text_grad(c):
        return dot_tn(PW[:, c * Q : (c + 1) * Q], HI[...]).reshape(4, R, W)

    def ct(c):
        half = pl.ds(c * 4, 4)
        return push(ST.at[half], CT.at[half], ct_s.at[c], ct_r.at[c], sib)

    near_t = {1: push(S2.at[0], RT.at[0], rt_s.at[0], rt_r.at[0], at_z(-1)),
              7: push(S2.at[1], RT.at[1], rt_s.at[1], rt_r.at[1], at_z(1))}
    relay_t = {3: push(S2.at[2], RA.at[0], ra_s.at[0], ra_r.at[0], at_z(-1)),
               5: push(S2.at[3], RA.at[1], ra_s.at[1], ra_r.at[1], at_z(1))}
    half_t = [push(S2.at[4, pl.ds(n * H, H)], RB.at[n], rb_s.at[n], rb_r.at[n], at_z(2 * (2 * n - 1))) for n in (0, 1)]
    sum_t = [push(RM.at[n], RT.at[2 + n], rt_s.at[2 + n], rt_r.at[2 + n], at_z(2 * (2 * n - 1))) for n in (0, 1)]

    def both(d):
        n = POS[d] if POS[d] < 4 else POS[d] - 4
        return GT[n] + CT[n].astype(F32)

    pair(0, 2)
    ST[0:4] = text_grad(1).astype(BF)
    ct(0).start()
    GT[0:4] = text_grad(0)
    pair(2, 2)
    ct(0).wait_recv()
    S2[4] = both(4).astype(BF)
    half_t[0].start()
    half_t[1].start()
    S2[2] = both(3).astype(BF)
    relay_t[3].start()
    S2[3] = both(5).astype(BF)
    relay_t[5].start()
    ST[4:8] = text_grad(3).astype(BF)
    ct(1).start()

    def r1(d):
        return push(SI.at[d, 1:4, pl.ds(0, H)], R1.at[d, 1:4], r1_s.at[d], r1_r.at[d], at_y(-d))

    def r2(d):
        return push(SI.at[1:4, d, pl.ds(H, H)], R2.at[d, 1:4], r2_s.at[d], r2_r.at[d], at_x(-d))

    def e1(d):
        return push(SI.at[d, 0, pl.ds(0, H)], R1.at[d, 0], e1_s.at[d], e1_r.at[d], at_y(-d))

    def e2(d):
        return push(SI.at[0, d, pl.ds(H, H)], R2.at[d, 0], e2_s.at[d], e2_r.at[d], at_x(-d))

    SI[...] = dot(PW[...], HT[...]).astype(BF).reshape(4, 4, R, W)
    for d in (2, 1, 3):
        r1(d).start()
        r2(d).start()
    for d in (2, 1, 3):
        e1(d).start()
        e2(d).start()

    GT[4:8] = text_grad(2)
    ct(1).wait_recv()
    S2[0] = both(1).astype(BF)
    near_t[1].start()
    S2[1] = both(7).astype(BF)
    near_t[7].start()

    for n, (d_near, d_far) in enumerate(((2, 3), (6, 5))):
        relay_t[d_far].wait_recv()
        half_t[n].wait_recv()
        m = both(d_near) + RA[n].astype(F32)
        extra = RB[n].astype(F32)
        rows, rest = (slice(0, H), slice(H, R)) if n == 0 else (slice(H, R), slice(0, H))
        RM[n, rows] = (m[rows] + extra).astype(BF)
        RM[n, rest] = m[rest].astype(BF)
        sum_t[n].start()

    def flip(j):
        lanes = pl.ds(pl.multiple_of(j * Q, Q), Q)
        XIT[lanes] = XI[:, :, :, lanes].reshape(B, Q).T
        XTT[lanes] = XT[:, :, lanes].reshape(B, Q).T

    each(0, NB, flip)

    def f1(d):
        return push(N1.at[d], F1.at[d], f1_s.at[d], f1_r.at[d], at_x(-d))

    def f2(d):
        return push(N2.at[d], F2.at[d], f2_s.at[d], f2_r.at[d], at_y(-d))

    arrived(r1(d) for d in (1, 3, 2))

    def sum1(d):
        N1[d] = (SI[0, d, 0:H].astype(F32) + R1[1, d].astype(F32) + R1[2, d].astype(F32) + R1[3, d].astype(F32)).astype(BF)

    def sum2(d):
        N2[d] = (SI[d, 0, H:R].astype(F32) + R2[1, d].astype(F32) + R2[2, d].astype(F32) + R2[3, d].astype(F32)).astype(BF)

    for d in (2, 1, 3):
        sum1(d)
        f1(d).start()
    arrived(r2(d) for d in (1, 3, 2))
    for d in (2, 1, 3):
        sum2(d)
        f2(d).start()

    def unembed(g, D, L, blocks):
        d = D[...]
        half = ((g - d * jnp.sum(d * g, axis=1, keepdims=True)) / L[...]).astype(BF)
        for j in range(NB):
            blocks[j] = half[:, j * Q : (j + 1) * Q]
        return half

    arrived((near_t[1], near_t[7], sum_t[0], sum_t[1]))
    g = both(0)
    for n in range(4):
        g = g + RT[n].astype(F32)
    half_text = unembed(g, DT, LT, TB)
    mine = jnp.where(k == 0, z, 8)

    def pt(s):
        zz = rem(z + s % 8, 8)
        kk = rem(k + s // 8, 2)
        slot = POS[s % 8] + 4 * (s // 8)
        return push(TB.at[jnp.where(kk == 0, zz, 8)], PT.at[slot], pt_s.at[s], pt_r.at[s], device(zz, y, x, kk))

    for s in range(1, 16):
        pt(s).start()
    PT[OWN] = TB[mine]

    arrived(e1(d) for d in (1, 3, 2))
    sum1(0)
    arrived(e2(d) for d in (1, 3, 2))
    sum2(0)
    arrived(f1(d) for d in (1, 3, 2))
    arrived(f2(d) for d in (1, 3, 2))
    g1 = N1[0].astype(F32)
    g2 = N2[0].astype(F32)
    for d in (1, 2, 3):
        g1 = g1 + F1[d].astype(F32)
        g2 = g2 + F2[d].astype(F32)
    half_image = unembed(jnp.concatenate([g1, g2], axis=0), DI, LI, GB)

    def plane_index(i):
        return rem(y + div(i, 4), 4) * 4 + rem(x + rem(i, 4), 4)

    def pi(i, block=None):
        block = plane_index(i) if block is None else block
        to = device(z, rem(y + div(i, 4), 4), rem(x + rem(i, 4), 4), k)
        return push(GB.at[block], PI.at[i], pi_s.at[i], pi_r.at[i], to)

    def pi_send(i):
        @pl.when(plane_index(i) < NB)
        def _():
            pi(i).start()

    each(1, 16, pi_send)
    sums_image = p0 < NB

    for s in range(1, 16):
        pt(s).wait_recv()
    PART[...] = dot(XTT[...], PT[...].reshape(B, Q))
    m, h = 2 * y + rem(x, 2), div(x, 2)
    zt = rem(m + 8 - z, 8)
    sums_text = (k == 0) | (m == z)

    def ut_place(u):
        return jnp.where(k == 0, rem(div(u, 2) + z, 8), z)

    def ut(u):
        at = ut_place(u)
        to = device(z, div(at, 2), 2 * rem(u, 2) + rem(at, 2), k)
        return push(VB.at[u], UT.at[p0], ut_s.at[u], ut_r.at[p0], to)

    def ut_here(u):
        return (ut_place(u) == m) & (rem(u, 2) == h)

    def ut_used(u):
        return (k == 0) | (div(u, 2) == z)

    def ut_send(i):
        u = rem(i + 2 * zt + 8, 16)

        @pl.when(ut_used(u))
        def _():
            VB[u, 0:U] = PART[pl.ds(pl.multiple_of(u * U, 8), U)].astype(BF)

            @pl.when(ut_here(u))
            def _():
                UT[p0] = VB[u]

            @pl.when(jnp.logical_not(ut_here(u)))
            def _():
                ut(u).start()

    each(0, 16, ut_send)

    def cb():
        return push(SB, CB, cb_s.at[0], cb_r.at[0], sib)

    def ui(d):
        return push(UB.at[d], UI.at[d], ui_s.at[d], ui_r.at[d], device(rem(z + d, 8), y, x, k))

    def head_rows(zz, h):
        return pl.ds(pl.multiple_of(zz * (2 * U) + h * U, 8), U)

    @pl.when(sums_image)
    def _():
        PI[0] = GB[p0]
        each(1, 16, lambda i: pi(i, 0).wait_recv())
        PARI[...] = dot(XIT[...], PI[...].reshape(B, Q))

        def give(d):
            SB[d, 0:U] = PARI[head_rows(rem(z + d, 8), 1 - k)].astype(BF)

        each(0, 8, give)
        cb().start()

    out[R : 2 * R] = dot_nt(half_text, WT[...])

    @pl.when(sums_image)
    def _():
        cb().wait_recv()

        def pass_on(i):
            d = rem(i + 4, 8)
            UB[d, 0:U] = (PARI[head_rows(rem(z + d, 8), k)] + CB[d, 0:U].astype(F32)).astype(BF)

            @pl.when(d > 0)
            def _():
                ui(d).start()

        each(0, 8, pass_on)

    for copy in (*z_near.values(), *z_far.values(), *near_t.values(), *relay_t.values(), *half_t, *sum_t):
        copy.wait_send()
    for n in POS.values():
        ac(n).wait_send()
    for copy in (a1, a2):
        for d in (1, 2, 3):
            for e in (1, 2, 3):
                copy(d, e).wait_send()
    for copy in (ax, ay, r1, r2, e1, e2, f1, f2):
        for d in (1, 2, 3):
            copy(d).wait_send()
    ct(0).wait_send()
    ct(1).wait_send()
    for s in range(1, 16):
        pt(s).wait_send()

    def pi_sent(i):
        @pl.when(plane_index(i) < NB)
        def _():
            pi(i, 0).wait_send()

    each(1, 16, pi_sent)

    block = jnp.where(k == 0, z, 8)
    zd = jnp.where(k == 0, zt, z)

    def ft(t):
        to = device(zd, rem(y + 2 + div(t, 4), 4), 2 * h + rem(div(t, 2), 2), rem(t, 2))
        return push(CX, FT.at[block], ft_s.at[t], ft_r.at[block], to)

    def ft_here(t):
        return (zd == z) & (div(t, 4) == 2) & (rem(div(t, 2), 2) == rem(x, 2)) & (rem(t, 2) == k)

    def fi(t):
        to = device(z, rem(y + 2 + div(t, 4), 4), k * 2 + rem(div(t, 2), 2), rem(t, 2))
        return push(CI, FI.at[p0], fi_s.at[t], fi_r.at[p0], to)

    def fi_here(t):
        return (div(t, 4) == 2) & (k * 2 + rem(div(t, 2), 2) == x) & (rem(t, 2) == k)

    @pl.when(sums_text)
    def _():
        def add_text(q, acc):
            @pl.when(q != p0)
            def _():
                push(VB.at[0], UT.at[q], ut_s.at[0], ut_r.at[q], sib).wait_recv()

            return acc + UT[q, 0:U].astype(F32)

        CX[0:U] = lax.fori_loop(0, 16, add_text, jnp.zeros((U, Q), F32)).astype(BF)

        def send(t):
            @pl.when(ft_here(t))
            def _():
                FT[block] = CX[...]

            @pl.when(jnp.logical_not(ft_here(t)))
            def _():
                ft(t).start()

        each(0, 16, send)

    out[0:R] = dot_nt(half_image, WI[...])

    @pl.when(sums_image)
    def _():
        def add_image(d, acc):
            ui(d).wait_recv()
            return acc + UI[d, 0:U].astype(F32)

        CI[0:U] = lax.fori_loop(1, 8, add_image, UB[0, 0:U].astype(F32)).astype(BF)

        def send(t):
            @pl.when(fi_here(t))
            def _():
                FI[p0] = CI[...]

            @pl.when(jnp.logical_not(fi_here(t)))
            def _():
                fi(t).start()

        each(0, 16, send)

    for j in range(NB):
        lanes = slice(j * Q, (j + 1) * Q)

        mine_j = ((k == 1) & (m == z)) if j == 8 else ((k == 0) & (z == j) & (zt == z))

        @pl.when(jnp.logical_not(mine_j))
        def _():
            push(CX, FT.at[j], ft_s.at[0], ft_r.at[j], sib).wait_recv()

        out[2 * R + U :, lanes] = FT[j, 0:U].astype(F32)

    for j in range(NB):
        lanes = slice(j * Q, (j + 1) * Q)

        @pl.when(jnp.logical_not((p0 == j) & (h == k)))
        def _():
            push(CI, FI.at[j], fi_s.at[0], fi_r.at[j], sib).wait_recv()

        out[2 * R : 2 * R + U, lanes] = FI[j, 0:U].astype(F32)

    def ut_sent(u):
        @pl.when(ut_used(u) & jnp.logical_not(ut_here(u)))
        def _():
            push(VB.at[0], UT.at[0], ut_s.at[u], ut_r.at[0], sib).wait_send()

    each(0, 16, ut_sent)

    @pl.when(sums_image)
    def _():
        cb().wait_send()
        each(1, 8, lambda d: ui(d).wait_send())

        def sent(t):
            @pl.when(jnp.logical_not(fi_here(t)))
            def _():
                push(CI, FI.at[0], fi_s.at[t], fi_r.at[0], sib).wait_send()

        each(0, 16, sent)

    @pl.when(sums_text)
    def _():
        def sent(t):
            @pl.when(jnp.logical_not(ft_here(t)))
            def _():
                push(CX, FT.at[0], ft_s.at[t], ft_r.at[0], sib).wait_send()

        each(0, 16, sent)


def body(image_features, text_features, image_weight, text_weight, log_scale, bias):
    vmem = pl.BlockSpec(memory_space=pltpu.VMEM)
    hbm = pl.BlockSpec(memory_space=pltpu.HBM)
    v = pltpu.VMEM
    dma = pltpu.SemaphoreType.DMA
    results = pl.pallas_call(
        kernel,
        out_shape=jax.ShapeDtypeStruct((2 * R + 2 * U, W), F32),
        in_specs=[hbm, hbm, hbm, vmem, vmem],
        out_specs=vmem,
        scratch_shapes=[
            v((W, W), BF), v((W, W), BF), v((4, 4, R, W), BF), v((16, R, W), BF), v((B, W), BF), v((B, W), BF), v((B, B), BF),
            v((W, B), BF), v((W, B), BF),
            v((R, W), F32), v((R, 1), F32), v((R, W), F32), v((R, 1), F32),
            v((8, R, W), BF), v((8, R, W), BF), v((8, R, W), F32), v((5, R, W), BF),
            v((2, R, W), BF), v((2, H, W), BF), v((2, R, W), BF), v((4, R, W), BF),
            v((4, 4, R, W), BF), v((4, 4, H, W), BF), v((4, 4, H, W), BF), v((4, H, W), BF), v((4, H, W), BF), v((4, H, W), BF), v((4, H, W), BF),
            v((NB, R, Q), BF), v((16, R, Q), BF), v((NB, R, Q), BF), v((16, R, Q), BF), v((W, Q), F32), v((W, Q), F32),
            v((8, UP, Q), BF), v((8, UP, Q), BF), v((8, UP, Q), BF), v((8, UP, Q), BF), v((16, UP, Q), BF), v((16, UP, Q), BF),
            v((UP, Q), BF), v((UP, Q), BF), v((NB, UP, Q), BF), v((NB, UP, Q), BF),
            dma((4,)), dma((8,)), dma((8,)), dma((12,)), dma((12,)), *[dma((4,)) for _ in range(4)], *[dma((16,)) for _ in range(4)],
            dma((2,)), dma((2,)), dma((2,)), dma((2,)), dma((2,)), dma((2,)), dma((4,)), dma((4,)), *[dma((4,)) for _ in range(12)],
            dma((16,)), dma((16,)), dma((16,)), dma((16,)), dma((1,)), dma((1,)), dma((8,)), dma((8,)),
            dma((16,)), dma((16,)), dma((16,)), dma((NB,)), dma((16,)), dma((NB,)),
        ],
        compiler_params=pltpu.CompilerParams(
            collective_id=0, has_side_effects=True, vmem_limit_bytes=52 * 1024 * 1024
        ),
    )(
        jnp.stack([image_features, text_features]), image_weight, text_weight,
        log_scale.reshape(1, 1), bias.reshape(1, 1),
    )

    return results[:R], results[R : 2 * R], results[2 * R : 2 * R + U], results[2 * R + U :]


def solution(mesh):
    in_specs = (P(("row", "col"), None), P(("col", "row"), None), P(), P(), P(), P())
    out_specs = (P(("row", "col"), None), P(("col", "row"), None), P("row", None), P("row", None))
    return jax.shard_map(body, mesh=mesh, in_specs=in_specs, out_specs=out_specs, check_vma=False)
```

```python
import jax
import jax.numpy as jnp
from jax import lax
from jax.experimental import pallas as pl
from jax.experimental.pallas import tpu as pltpu
from jax.sharding import PartitionSpec as P

MESH = pl.DeviceIdType.MESH
BF = jnp.bfloat16
F32 = jnp.float32
W = 1152
R = 32
H = 16
B = 512
Q = 128
U = 72
UP = 80
NB = 9
POS = {6: 0, 3: 1, 5: 2, 4: 3, 0: 8, 1: 9, 7: 10, 2: 11}
OWN = POS[0]


def div(a, b):
    return a // b if isinstance(a, int) else lax.div(a, jnp.int32(b))


def rem(a, b):
    return a % b if isinstance(a, int) else lax.rem(a, jnp.int32(b))


def place():
    r, c = lax.axis_index("row"), lax.axis_index("col")
    return div(r, 2), div(c, 4), rem(r, 2) * 2 + div(rem(c, 4), 2), rem(c, 2)


def device(z, y, x, k):
    return (z * 2 + div(x, 2), y * 4 + rem(x, 2) * 2 + k)


def push(src, dst, send, recv, to):
    return pltpu.make_async_remote_copy(
        src_ref=src, dst_ref=dst, send_sem=send, recv_sem=recv, device_id=to, device_id_type=MESH
    )


def dot(a, b):
    return jnp.dot(a, b, preferred_element_type=F32)


def dot_nt(a, b):
    return lax.dot_general(a, b, (((1,), (1,)), ((), ())), preferred_element_type=F32)


def dot_tn(a, b):
    return lax.dot_general(a, b, (((0,), (0,)), ((), ())), preferred_element_type=F32)


def each(lo, hi, fn):
    def step(i, carry):
        fn(i)
        return carry

    lax.fori_loop(lo, hi, step, 0)


def kernel(
    xi, xt, wi_hbm, wt_hbm, ls, bs,
    out,
    WI, WT, XI, XT, HI, HT, PW, XIT, XTT,
    DI, LI, DT, LT,
    ST, CT, GT, S2, RA, RB, RM, RT, SI, R1, R2, N1, N2, F1, F2,
    GB, PI, TB, PT, PARI, PART, SB, CB, UB, UI, VB, UT, CI, CX, FI, FT,
    lsem, at_s, at_r, ac_s, ac_r, ax_s, ax_r, ay_s, ay_r, a1_s, a1_r, a2_s, a2_r,
    ct_s, ct_r, ra_s, ra_r, rb_s, rb_r, rt_s, rt_r, r1_s, r1_r, r2_s, r2_r, e1_s, e1_r, e2_s, e2_r, f1_s, f1_r, f2_s, f2_r,
    pi_s, pi_r, pt_s, pt_r, cb_s, cb_r, ui_s, ui_r, ut_s, ut_r, fi_s, fi_r, ft_s, ft_r,
):
    z, y, x, k = place()
    p0 = y * 4 + x
    sib = device(z, y, x, 1 - k)

    def at_z(d):
        return device(rem(z + d + 8, 8), y, x, k)

    def at_y(d):
        return device(z, rem(y + d + 4, 4), x, k)

    def at_x(d):
        return device(z, y, rem(x + d + 4, 4), k)

    loads = [
        pltpu.make_async_copy(src, dst, lsem.at[n])
        for n, (src, dst) in enumerate(((xt, XT.at[OWN]), (xi, XI.at[0, 0]), (wt_hbm, WT), (wi_hbm, WI)))
    ]
    for load in loads:
        load.start()

    bar = pltpu.get_barrier_semaphore()
    near = [at_z(d) for d in (1, -1, 2, -2)] + [at_x(d) for d in (1, 2, 3)] + [at_y(d) for d in (1, 2, 3)] + [sib]
    for to in near:
        pl.semaphore_signal(bar, inc=1, device_id=to, device_id_type=MESH)

    pad = jnp.zeros((8, UP - U, Q), BF)
    for buf in (SB, UB, VB.at[0:8], VB.at[8:16]):
        buf[:, U:UP] = pad
    CI[U:UP] = pad[0]
    CX[U:UP] = pad[0]

    loads[0].wait()
    loads[1].wait()
    pl.semaphore_wait(bar, len(near))

    def tz(d, d_to, n, rows=None):
        src, dst = XT.at[POS[d % 8]], XT.at[POS[(d + d_to) % 8]]
        if rows is not None:
            src, dst = src.at[pl.ds(rows, H)], dst.at[pl.ds(rows, H)]
        return push(src, dst, at_s.at[n], at_r.at[n], at_z(d_to))

    z_near = {1: tz(0, 1, 0), 7: tz(0, -1, 1), 2: tz(0, 2, 2), 6: tz(0, -2, 3)}
    z_far = {3: tz(2, 1, 4), 5: tz(-2, -1, 5), 4: tz(2, 2, 6, 0), 12: tz(-2, -2, 7, H)}

    def ac(s):
        return push(XT.at[s], XT.at[s + 4], ac_s.at[s], ac_r.at[s], sib)

    def ax(d):
        return push(XI.at[0, 0], XI.at[0, d], ax_s.at[d], ax_r.at[d], at_x(d))

    def ay(d):
        return push(XI.at[0, 0], XI.at[d, 0], ay_s.at[d], ay_r.at[d], at_y(d))

    def a1(d):
        rows = pl.ds(0, H)
        return push(XI.at[0, 1:4, rows], XI.at[d, 1:4, rows], a1_s.at[d], a1_r.at[d], at_y(d))

    def a2(d):
        rows = pl.ds(H, H)
        return push(XI.at[1:4, 0, rows], XI.at[1:4, d, rows], a2_s.at[d], a2_r.at[d], at_x(d))

    z_near[2].start()
    z_near[6].start()
    for d in (2, 1, 3):
        ax(d).start()
        ay(d).start()
    z_near[1].start()
    z_near[7].start()
    ac(OWN).start()

    def project(x_in, n, WW, HH, c):
        p = dot(x_in.reshape(n * Q, W), WW[...])
        length = jnp.sqrt(jnp.sum(p * p, axis=1, keepdims=True) + 1e-06)
        p = p * (1.0 / length)
        HH[c * Q : (c + n) * Q] = p.astype(BF)
        return p, length

    def arrived(copies):
        for copy in copies:
            copy.wait_recv()

    z_near[2].wait_recv()
    z_far[4].start()
    z_far[3].start()
    ac(POS[2]).start()
    z_near[6].wait_recv()
    z_far[12].start()
    z_far[5].start()
    arrived(ax(d) for d in (1, 3, 2))
    for d in (2, 1, 3):
        a1(d).start()
    arrived(ay(d) for d in (1, 3, 2))
    for d in (2, 1, 3):
        a2(d).start()
    ac(POS[6]).start()
    for d in (1, 7):
        z_near[d].wait_recv()
        ac(POS[d]).start()

    loads[2].wait()
    p, length = project(XT[8:12], 1, WT, HT, 2)
    DT[...] = p[:R]
    LT[...] = length[:R]
    loads[3].wait()
    p, length = project(XI[0], 1, WI, HI, 0)
    DI[...] = p[:R]
    LI[...] = length[:R]

    arrived([z_far[3]])
    ac(POS[3]).start()
    arrived([z_far[5]])
    ac(POS[5]).start()
    arrived([z_far[4], z_far[12]])
    ac(POS[4]).start()
    arrived(ac(s) for s in (8, 9, 10, 11))
    project(XT[12:16], 1, WT, HT, 3)
    arrived(ac(s) for s in range(4))
    project(XT[0:8], 2, WT, HT, 0)
    arrived(a(d) for a in (a1, a2) for d in (1, 3, 2))
    project(XI[1:4], 3, WI, HI, 1)

    factor = jnp.exp(ls[...])
    bias = bs[...]
    col = lax.broadcasted_iota(jnp.int32, (1, B), 1)
    cs = col >> 5
    cd = jnp.zeros_like(cs)
    for d, n in POS.items():
        cd = jnp.where((cs & 11) == n, d, cd)
    cz = (z - cd) & 7
    ck = k ^ ((cs >> 2) & 1)
    tid = (y * 4 + rem(x, 2) * 2 + ck) * B + (cz * 2 + div(x, 2)) * R + (col & 31)
    row = lax.broadcasted_iota(jnp.int32, (B, 1), 0)
    rs = row >> 5
    ry = (y - (rs >> 2)) & 3
    rx = (x - (rs & 3)) & 3
    iid = (z * 2 + (rx >> 1)) * B + (ry * 4 + ((rx & 1) << 1) + k) * R + (row & 31)

    def pair(c, n):
        cols = slice(c * Q, (c + n) * Q)
        logits = factor * dot_nt(HI[...], HT[cols]) + bias
        same = iid == tid[:, cols]
        signed = jnp.where(same, -logits, logits)
        weight = factor / (1.0 + jnp.exp(-signed))
        PW[:, cols] = jnp.where(same, -weight, weight).astype(BF)

    def text_grad(c):
        return dot_tn(PW[:, c * Q : (c + 1) * Q], HI[...]).reshape(4, R, W)

    def ct(c):
        half = pl.ds(c * 4, 4)
        return push(ST.at[half], CT.at[half], ct_s.at[c], ct_r.at[c], sib)

    near_t = {1: push(S2.at[0], RT.at[0], rt_s.at[0], rt_r.at[0], at_z(-1)),
              7: push(S2.at[1], RT.at[1], rt_s.at[1], rt_r.at[1], at_z(1))}
    relay_t = {3: push(S2.at[2], RA.at[0], ra_s.at[0], ra_r.at[0], at_z(-1)),
               5: push(S2.at[3], RA.at[1], ra_s.at[1], ra_r.at[1], at_z(1))}
    half_t = [push(S2.at[4, pl.ds(n * H, H)], RB.at[n], rb_s.at[n], rb_r.at[n], at_z(2 * (2 * n - 1))) for n in (0, 1)]
    sum_t = [push(RM.at[n], RT.at[2 + n], rt_s.at[2 + n], rt_r.at[2 + n], at_z(2 * (2 * n - 1))) for n in (0, 1)]

    def both(d):
        n = POS[d] if POS[d] < 4 else POS[d] - 4
        return GT[n] + CT[n].astype(F32)

    pair(0, 2)
    ST[0:4] = text_grad(1).astype(BF)
    ct(0).start()
    GT[0:4] = text_grad(0)
    pair(2, 2)
    ct(0).wait_recv()
    S2[4] = both(4).astype(BF)
    half_t[0].start()
    half_t[1].start()
    S2[2] = both(3).astype(BF)
    relay_t[3].start()
    S2[3] = both(5).astype(BF)
    relay_t[5].start()
    ST[4:8] = text_grad(3).astype(BF)
    ct(1).start()

    def r1(d):
        return push(SI.at[d, 1:4, pl.ds(0, H)], R1.at[d, 1:4], r1_s.at[d], r1_r.at[d], at_y(-d))

    def r2(d):
        return push(SI.at[1:4, d, pl.ds(H, H)], R2.at[d, 1:4], r2_s.at[d], r2_r.at[d], at_x(-d))

    def e1(d):
        return push(SI.at[d, 0, pl.ds(0, H)], R1.at[d, 0], e1_s.at[d], e1_r.at[d], at_y(-d))

    def e2(d):
        return push(SI.at[0, d, pl.ds(H, H)], R2.at[d, 0], e2_s.at[d], e2_r.at[d], at_x(-d))

    SI[...] = dot(PW[...], HT[...]).astype(BF).reshape(4, 4, R, W)
    for d in (2, 1, 3):
        r1(d).start()
        r2(d).start()
    for d in (2, 1, 3):
        e1(d).start()
        e2(d).start()

    GT[4:8] = text_grad(2)
    ct(1).wait_recv()
    S2[0] = both(1).astype(BF)
    near_t[1].start()
    S2[1] = both(7).astype(BF)
    near_t[7].start()

    for n, (d_near, d_far) in enumerate(((2, 3), (6, 5))):
        relay_t[d_far].wait_recv()
        half_t[n].wait_recv()
        m = both(d_near) + RA[n].astype(F32)
        extra = RB[n].astype(F32)
        rows, rest = (slice(0, H), slice(H, R)) if n == 0 else (slice(H, R), slice(0, H))
        RM[n, rows] = (m[rows] + extra).astype(BF)
        RM[n, rest] = m[rest].astype(BF)
        sum_t[n].start()

    def flip(j):
        lanes = pl.ds(pl.multiple_of(j * Q, Q), Q)
        XIT[lanes] = XI[:, :, :, lanes].reshape(B, Q).T
        XTT[lanes] = XT[:, :, lanes].reshape(B, Q).T

    each(0, NB, flip)

    def f1(d):
        return push(N1.at[d], F1.at[d], f1_s.at[d], f1_r.at[d], at_x(-d))

    def f2(d):
        return push(N2.at[d], F2.at[d], f2_s.at[d], f2_r.at[d], at_y(-d))

    arrived(r1(d) for d in (1, 3, 2))

    def sum1(d):
        N1[d] = (SI[0, d, 0:H].astype(F32) + R1[1, d].astype(F32) + R1[2, d].astype(F32) + R1[3, d].astype(F32)).astype(BF)

    def sum2(d):
        N2[d] = (SI[d, 0, H:R].astype(F32) + R2[1, d].astype(F32) + R2[2, d].astype(F32) + R2[3, d].astype(F32)).astype(BF)

    for d in (2, 1, 3):
        sum1(d)
        f1(d).start()
    arrived(r2(d) for d in (1, 3, 2))
    for d in (2, 1, 3):
        sum2(d)
        f2(d).start()

    def unembed(g, D, L, blocks):
        d = D[...]
        half = ((g - d * jnp.sum(d * g, axis=1, keepdims=True)) / L[...]).astype(BF)
        for j in range(NB):
            blocks[j] = half[:, j * Q : (j + 1) * Q]
        return half

    arrived((near_t[1], near_t[7], sum_t[0], sum_t[1]))
    g = both(0)
    for n in range(4):
        g = g + RT[n].astype(F32)
    half_text = unembed(g, DT, LT, TB)
    mine = jnp.where(k == 0, z, 8)

    def pt(s):
        zz = rem(z + s % 8, 8)
        kk = rem(k + s // 8, 2)
        slot = POS[s % 8] + 4 * (s // 8)
        return push(TB.at[jnp.where(kk == 0, zz, 8)], PT.at[slot], pt_s.at[s], pt_r.at[s], device(zz, y, x, kk))

    for s in (12, 11, 13, 4, 3, 5, 10, 14, 2, 6, 9, 15, 1, 7, 8):
        pt(s).start()
    PT[OWN] = TB[mine]

    arrived(e1(d) for d in (1, 3, 2))
    sum1(0)
    arrived(e2(d) for d in (1, 3, 2))
    sum2(0)
    arrived(f1(d) for d in (1, 3, 2))
    arrived(f2(d) for d in (1, 3, 2))
    g1 = N1[0].astype(F32)
    g2 = N2[0].astype(F32)
    for d in (1, 2, 3):
        g1 = g1 + F1[d].astype(F32)
        g2 = g2 + F2[d].astype(F32)
    half_image = unembed(jnp.concatenate([g1, g2], axis=0), DI, LI, GB)

    def plane_index(i):
        return rem(y + div(i, 4), 4) * 4 + rem(x + rem(i, 4), 4)

    def pi(i, block=None):
        block = plane_index(i) if block is None else block
        to = device(z, rem(y + div(i, 4), 4), rem(x + rem(i, 4), 4), k)
        return push(GB.at[block], PI.at[i], pi_s.at[i], pi_r.at[i], to)

    def pi_send(i):
        @pl.when(plane_index(i) < NB)
        def _():
            pi(i).start()

    each(1, 16, pi_send)
    sums_image = p0 < NB

    for s in range(1, 16):
        pt(s).wait_recv()
    PART[...] = dot(XTT[...], PT[...].reshape(B, Q))
    m, h = 2 * y + rem(x, 2), div(x, 2)
    zt = rem(m + 8 - z, 8)
    sums_text = (k == 0) | (m == z)

    def ut_place(u):
        return jnp.where(k == 0, rem(div(u, 2) + z, 8), z)

    def ut(u):
        at = ut_place(u)
        to = device(z, div(at, 2), 2 * rem(u, 2) + rem(at, 2), k)
        return push(VB.at[u], UT.at[p0], ut_s.at[u], ut_r.at[p0], to)

    def ut_here(u):
        return (ut_place(u) == m) & (rem(u, 2) == h)

    def ut_used(u):
        return (k == 0) | (div(u, 2) == z)

    def ut_send(i):
        u = rem(i + 2 * zt + 6, 16)

        @pl.when(ut_used(u))
        def _():
            VB[u, 0:U] = PART[pl.ds(pl.multiple_of(u * U, 8), U)].astype(BF)

            @pl.when(ut_here(u))
            def _():
                UT[p0] = VB[u]

            @pl.when(jnp.logical_not(ut_here(u)))
            def _():
                ut(u).start()

    each(0, 16, ut_send)

    def cb():
        return push(SB, CB, cb_s.at[0], cb_r.at[0], sib)

    def ui(d):
        return push(UB.at[d], UI.at[d], ui_s.at[d], ui_r.at[d], device(rem(z + d, 8), y, x, k))

    def head_rows(zz, h):
        return pl.ds(pl.multiple_of(zz * (2 * U) + h * U, 8), U)

    @pl.when(sums_image)
    def _():
        PI[0] = GB[p0]
        each(1, 16, lambda i: pi(i, 0).wait_recv())
        PARI[...] = dot(XIT[...], PI[...].reshape(B, Q))

        def give(d):
            SB[d, 0:U] = PARI[head_rows(rem(z + d, 8), 1 - k)].astype(BF)

        each(0, 8, give)
        cb().start()

    out[R : 2 * R] = dot_nt(half_text, WT[...])

    @pl.when(sums_image)
    def _():
        cb().wait_recv()

        def pass_on(i):
            d = rem(i + 4, 8)
            UB[d, 0:U] = (PARI[head_rows(rem(z + d, 8), k)] + CB[d, 0:U].astype(F32)).astype(BF)

            @pl.when(d > 0)
            def _():
                ui(d).start()

        each(0, 8, pass_on)

    for copy in (*z_near.values(), *z_far.values(), *near_t.values(), *relay_t.values(), *half_t, *sum_t):
        copy.wait_send()
    for n in POS.values():
        ac(n).wait_send()
    for copy in (ax, ay, a1, a2, r1, r2, e1, e2, f1, f2):
        for d in (1, 2, 3):
            copy(d).wait_send()
    ct(0).wait_send()
    ct(1).wait_send()
    for s in range(1, 16):
        pt(s).wait_send()

    def pi_sent(i):
        @pl.when(plane_index(i) < NB)
        def _():
            pi(i, 0).wait_send()

    each(1, 16, pi_sent)

    block = jnp.where(k == 0, z, 8)
    zd = jnp.where(k == 0, zt, z)

    def ft(t):
        to = device(zd, rem(y + 2 + div(t, 4), 4), 2 * h + rem(div(t, 2), 2), rem(t, 2))
        return push(CX, FT.at[block], ft_s.at[t], ft_r.at[block], to)

    def ft_here(t):
        return (zd == z) & (div(t, 4) == 2) & (rem(div(t, 2), 2) == rem(x, 2)) & (rem(t, 2) == k)

    def fi(t):
        to = device(z, rem(y + 2 + div(t, 4), 4), k * 2 + rem(div(t, 2), 2), rem(t, 2))
        return push(CI, FI.at[p0], fi_s.at[t], fi_r.at[p0], to)

    def fi_here(t):
        return (div(t, 4) == 2) & (k * 2 + rem(div(t, 2), 2) == x) & (rem(t, 2) == k)

    @pl.when(sums_text)
    def _():
        def add_text(q, acc):
            @pl.when(q != p0)
            def _():
                push(VB.at[0], UT.at[q], ut_s.at[0], ut_r.at[q], sib).wait_recv()

            return acc + UT[q, 0:U].astype(F32)

        CX[0:U] = lax.fori_loop(0, 16, add_text, jnp.zeros((U, Q), F32)).astype(BF)

        def send(t):
            @pl.when(ft_here(t))
            def _():
                FT[block] = CX[...]

            @pl.when(jnp.logical_not(ft_here(t)))
            def _():
                ft(t).start()

        each(0, 16, send)

    out[0:R] = dot_nt(half_image, WI[...])

    @pl.when(sums_image)
    def _():
        def add_image(d, acc):
            ui(d).wait_recv()
            return acc + UI[d, 0:U].astype(F32)

        CI[0:U] = lax.fori_loop(1, 8, add_image, UB[0, 0:U].astype(F32)).astype(BF)

        def send(t):
            @pl.when(fi_here(t))
            def _():
                FI[p0] = CI[...]

            @pl.when(jnp.logical_not(fi_here(t)))
            def _():
                fi(t).start()

        each(0, 16, send)

    for j in range(NB):
        lanes = slice(j * Q, (j + 1) * Q)

        mine_j = ((k == 1) & (m == z)) if j == 8 else ((k == 0) & (z == j) & (zt == z))

        @pl.when(jnp.logical_not(mine_j))
        def _():
            push(CX, FT.at[j], ft_s.at[0], ft_r.at[j], sib).wait_recv()

        out[2 * R + U :, lanes] = FT[j, 0:U].astype(F32)

    def ut_sent(u):
        @pl.when(ut_used(u) & jnp.logical_not(ut_here(u)))
        def _():
            push(VB.at[0], UT.at[0], ut_s.at[u], ut_r.at[0], sib).wait_send()

    each(0, 16, ut_sent)

    @pl.when(sums_image)
    def _():
        cb().wait_send()
        each(1, 8, lambda d: ui(d).wait_send())

    @pl.when(sums_text)
    def _():
        def sent(t):
            @pl.when(jnp.logical_not(ft_here(t)))
            def _():
                push(CX, FT.at[0], ft_s.at[t], ft_r.at[0], sib).wait_send()

        each(0, 16, sent)

    for j in range(NB):
        lanes = slice(j * Q, (j + 1) * Q)

        @pl.when(jnp.logical_not((p0 == j) & (h == k)))
        def _():
            push(CI, FI.at[j], fi_s.at[0], fi_r.at[j], sib).wait_recv()

        out[2 * R : 2 * R + U, lanes] = FI[j, 0:U].astype(F32)

    @pl.when(sums_image)
    def _():
        def sent(t):
            @pl.when(jnp.logical_not(fi_here(t)))
            def _():
                push(CI, FI.at[0], fi_s.at[t], fi_r.at[0], sib).wait_send()

        each(0, 16, sent)


def body(image_features, text_features, image_weight, text_weight, log_scale, bias):
    vmem = pl.BlockSpec(memory_space=pltpu.VMEM)
    hbm = pl.BlockSpec(memory_space=pltpu.HBM)
    v = pltpu.VMEM
    dma = pltpu.SemaphoreType.DMA
    results = pl.pallas_call(
        kernel,
        out_shape=jax.ShapeDtypeStruct((2 * R + 2 * U, W), F32),
        in_specs=[hbm, hbm, hbm, hbm, vmem, vmem],
        out_specs=vmem,
        scratch_shapes=[
            v((W, W), BF), v((W, W), BF), v((4, 4, R, W), BF), v((16, R, W), BF), v((B, W), BF), v((B, W), BF), v((B, B), BF),
            v((W, B), BF), v((W, B), BF),
            v((R, W), F32), v((R, 1), F32), v((R, W), F32), v((R, 1), F32),
            v((8, R, W), BF), v((8, R, W), BF), v((8, R, W), F32), v((5, R, W), BF),
            v((2, R, W), BF), v((2, H, W), BF), v((2, R, W), BF), v((4, R, W), BF),
            v((4, 4, R, W), BF), v((4, 4, H, W), BF), v((4, 4, H, W), BF), v((4, H, W), BF), v((4, H, W), BF), v((4, H, W), BF), v((4, H, W), BF),
            v((NB, R, Q), BF), v((16, R, Q), BF), v((NB, R, Q), BF), v((16, R, Q), BF), v((W, Q), F32), v((W, Q), F32),
            v((8, UP, Q), BF), v((8, UP, Q), BF), v((8, UP, Q), BF), v((8, UP, Q), BF), v((16, UP, Q), BF), v((16, UP, Q), BF),
            v((UP, Q), BF), v((UP, Q), BF), v((NB, UP, Q), BF), v((NB, UP, Q), BF),
            dma((4,)), dma((8,)), dma((8,)), dma((12,)), dma((12,)), *[dma((4,)) for _ in range(8)],
            dma((2,)), dma((2,)), dma((2,)), dma((2,)), dma((2,)), dma((2,)), dma((4,)), dma((4,)), *[dma((4,)) for _ in range(12)],
            dma((16,)), dma((16,)), dma((16,)), dma((16,)), dma((1,)), dma((1,)), dma((8,)), dma((8,)),
            dma((16,)), dma((16,)), dma((16,)), dma((NB,)), dma((16,)), dma((NB,)),
        ],
        compiler_params=pltpu.CompilerParams(
            collective_id=0, has_side_effects=True, vmem_limit_bytes=52 * 1024 * 1024
        ),
    )(
        pltpu.with_memory_space_constraint(image_features, pltpu.HBM), pltpu.with_memory_space_constraint(text_features, pltpu.HBM), image_weight, text_weight,
        log_scale.reshape(1, 1), bias.reshape(1, 1),
    )

    return results[:R], results[R : 2 * R], results[2 * R : 2 * R + U], results[2 * R + U :]


def solution(mesh):
    in_specs = (P(("row", "col"), None), P(("col", "row"), None), P(), P(), P(), P())
    out_specs = (P(("row", "col"), None), P(("col", "row"), None), P("row", None), P("row", None))
    return jax.shard_map(body, mesh=mesh, in_specs=in_specs, out_specs=out_specs, check_vma=False)
```

```python
import jax
import jax.numpy as jnp
from jax import lax
from jax.experimental import pallas as pl
from jax.experimental.pallas import tpu as pltpu
from jax.sharding import PartitionSpec as P

MESH = pl.DeviceIdType.MESH
BF = jnp.bfloat16
F32 = jnp.float32
W = 1152
R = 32
H = 16
B = 512
Q = 128
U = 72
UP = 80
NB = 9
POS = {6: 0, 3: 1, 5: 2, 4: 3, 0: 8, 1: 9, 7: 10, 2: 11}
OWN = POS[0]


def div(a, b):
    return a // b if isinstance(a, int) else lax.div(a, jnp.int32(b))


def rem(a, b):
    return a % b if isinstance(a, int) else lax.rem(a, jnp.int32(b))


def place():
    r, c = lax.axis_index("row"), lax.axis_index("col")
    return div(r, 2), div(c, 4), rem(r, 2) * 2 + div(rem(c, 4), 2), rem(c, 2)


def device(z, y, x, k):
    return (z * 2 + div(x, 2), y * 4 + rem(x, 2) * 2 + k)


def push(src, dst, send, recv, to):
    return pltpu.make_async_remote_copy(
        src_ref=src, dst_ref=dst, send_sem=send, recv_sem=recv, device_id=to, device_id_type=MESH
    )


def dot(a, b):
    return jnp.dot(a, b, preferred_element_type=F32)


def dot_nt(a, b):
    return lax.dot_general(a, b, (((1,), (1,)), ((), ())), preferred_element_type=F32)


def dot_tn(a, b):
    return lax.dot_general(a, b, (((0,), (0,)), ((), ())), preferred_element_type=F32)


def each(lo, hi, fn):
    def step(i, carry):
        fn(i)
        return carry

    lax.fori_loop(lo, hi, step, 0)


def kernel(
    xi, xt, wi_hbm, wt_hbm, ls, bs,
    out,
    WI, WT, XI, XT, HI, HT, PW, XIT, XTT,
    DI, LI, DT, LT,
    ST, CT, GT, S2, RA, RB, RM, RT, SI, R1, R2, N1, N2, F1, F2,
    GB, PI, TB, PT, PARI, PART, SB, CB, UB, UI, VB, UT, CI, CX, FI, FT,
    lsem, at_s, at_r, ac_s, ac_r, ax_s, ax_r, ay_s, ay_r, a1_s, a1_r, a2_s, a2_r,
    ct_s, ct_r, ra_s, ra_r, rb_s, rb_r, rt_s, rt_r, r1_s, r1_r, r2_s, r2_r, e1_s, e1_r, e2_s, e2_r, f1_s, f1_r, f2_s, f2_r,
    pi_s, pi_r, pt_s, pt_r, cb_s, cb_r, ui_s, ui_r, ut_s, ut_r, fi_s, fi_r, ft_s, ft_r, fo_s, fp_s,
):
    z, y, x, k = place()
    p0 = y * 4 + x
    sib = device(z, y, x, 1 - k)

    def at_z(d):
        return device(rem(z + d + 8, 8), y, x, k)

    def at_y(d):
        return device(z, rem(y + d + 4, 4), x, k)

    def at_x(d):
        return device(z, y, rem(x + d + 4, 4), k)

    loads = [
        pltpu.make_async_copy(src, dst, lsem.at[n])
        for n, (src, dst) in enumerate(((xt, XT.at[OWN]), (xi, XI.at[0, 0]), (wt_hbm, WT), (wi_hbm, WI)))
    ]
    for load in loads:
        load.start()

    bar = pltpu.get_barrier_semaphore()
    near = [at_z(d) for d in (1, -1, 2, -2)] + [at_x(d) for d in (1, 2, 3)] + [at_y(d) for d in (1, 2, 3)] + [sib]
    for to in near:
        pl.semaphore_signal(bar, inc=1, device_id=to, device_id_type=MESH)

    pad = jnp.zeros((8, UP - U, Q), BF)
    for buf in (SB, UB, VB.at[0:8], VB.at[8:16]):
        buf[:, U:UP] = pad
    CI[U:UP] = pad[0]
    CX[U:UP] = pad[0]

    loads[0].wait()
    loads[1].wait()
    pl.semaphore_wait(bar, len(near))

    def tz(d, d_to, n, rows=None):
        src, dst = XT.at[POS[d % 8]], XT.at[POS[(d + d_to) % 8]]
        if rows is not None:
            src, dst = src.at[pl.ds(rows, H)], dst.at[pl.ds(rows, H)]
        return push(src, dst, at_s.at[n], at_r.at[n], at_z(d_to))

    z_near = {1: tz(0, 1, 0), 7: tz(0, -1, 1), 2: tz(0, 2, 2), 6: tz(0, -2, 3)}
    z_far = {3: tz(2, 1, 4), 5: tz(-2, -1, 5), 4: tz(2, 2, 6, 0), 12: tz(-2, -2, 7, H)}

    def ac(s):
        return push(XT.at[s], XT.at[s + 4], ac_s.at[s], ac_r.at[s], sib)

    def ax(d):
        return push(XI.at[0, 0], XI.at[0, d], ax_s.at[d], ax_r.at[d], at_x(d))

    def ay(d):
        return push(XI.at[0, 0], XI.at[d, 0], ay_s.at[d], ay_r.at[d], at_y(d))

    def a1(d):
        rows = pl.ds(0, H)
        return push(XI.at[0, 1:4, rows], XI.at[d, 1:4, rows], a1_s.at[d], a1_r.at[d], at_y(d))

    def a2(d):
        rows = pl.ds(H, H)
        return push(XI.at[1:4, 0, rows], XI.at[1:4, d, rows], a2_s.at[d], a2_r.at[d], at_x(d))

    z_near[2].start()
    z_near[6].start()
    for d in (2, 1, 3):
        ax(d).start()
        ay(d).start()
    z_near[1].start()
    z_near[7].start()
    ac(OWN).start()

    def project(x_in, n, WW, HH, c):
        p = dot(x_in.reshape(n * Q, W), WW[...])
        length = jnp.sqrt(jnp.sum(p * p, axis=1, keepdims=True) + 1e-06)
        p = p * (1.0 / length)
        HH[c * Q : (c + n) * Q] = p.astype(BF)
        return p, length

    def arrived(copies):
        for copy in copies:
            copy.wait_recv()

    z_near[2].wait_recv()
    z_far[4].start()
    z_far[3].start()
    ac(POS[2]).start()
    z_near[6].wait_recv()
    z_far[12].start()
    z_far[5].start()
    arrived(ax(d) for d in (1, 3, 2))
    for d in (2, 1, 3):
        a1(d).start()
    arrived(ay(d) for d in (1, 3, 2))
    for d in (2, 1, 3):
        a2(d).start()
    ac(POS[6]).start()
    for d in (1, 7):
        z_near[d].wait_recv()
        ac(POS[d]).start()

    loads[2].wait()
    p, length = project(XT[8:12], 1, WT, HT, 2)
    DT[...] = p[:R]
    LT[...] = length[:R]
    loads[3].wait()
    p, length = project(XI[0], 1, WI, HI, 0)
    DI[...] = p[:R]
    LI[...] = length[:R]

    arrived([z_far[3]])
    ac(POS[3]).start()
    arrived([z_far[5]])
    ac(POS[5]).start()
    arrived([z_far[4], z_far[12]])
    ac(POS[4]).start()
    arrived(ac(s) for s in (8, 9, 10, 11))
    project(XT[12:16], 1, WT, HT, 3)
    arrived(ac(s) for s in range(4))
    project(XT[0:8], 2, WT, HT, 0)
    arrived(a(d) for a in (a1, a2) for d in (1, 3, 2))
    project(XI[1:4], 3, WI, HI, 1)

    factor = jnp.exp(ls[...])
    bias = bs[...]
    col = lax.broadcasted_iota(jnp.int32, (1, B), 1)
    cs = col >> 5
    cd = jnp.zeros_like(cs)
    for d, n in POS.items():
        cd = jnp.where((cs & 11) == n, d, cd)
    cz = (z - cd) & 7
    ck = k ^ ((cs >> 2) & 1)
    tid = (y * 4 + rem(x, 2) * 2 + ck) * B + (cz * 2 + div(x, 2)) * R + (col & 31)
    row = lax.broadcasted_iota(jnp.int32, (B, 1), 0)
    rs = row >> 5
    ry = (y - (rs >> 2)) & 3
    rx = (x - (rs & 3)) & 3
    iid = (z * 2 + (rx >> 1)) * B + (ry * 4 + ((rx & 1) << 1) + k) * R + (row & 31)

    def pair(c, n):
        cols = slice(c * Q, (c + n) * Q)
        logits = factor * dot_nt(HI[...], HT[cols]) + bias
        same = iid == tid[:, cols]
        signed = jnp.where(same, -logits, logits)
        weight = factor / (1.0 + jnp.exp(-signed))
        PW[:, cols] = jnp.where(same, -weight, weight).astype(BF)

    def text_grad(c):
        return dot_tn(PW[:, c * Q : (c + 1) * Q], HI[...]).reshape(4, R, W)

    def ct(c):
        half = pl.ds(c * 4, 4)
        return push(ST.at[half], CT.at[half], ct_s.at[c], ct_r.at[c], sib)

    near_t = {1: push(S2.at[0], RT.at[0], rt_s.at[0], rt_r.at[0], at_z(-1)),
              7: push(S2.at[1], RT.at[1], rt_s.at[1], rt_r.at[1], at_z(1))}
    relay_t = {3: push(S2.at[2], RA.at[0], ra_s.at[0], ra_r.at[0], at_z(-1)),
               5: push(S2.at[3], RA.at[1], ra_s.at[1], ra_r.at[1], at_z(1))}
    half_t = [push(S2.at[4, pl.ds(n * H, H)], RB.at[n], rb_s.at[n], rb_r.at[n], at_z(2 * (2 * n - 1))) for n in (0, 1)]
    sum_t = [push(RM.at[n], RT.at[2 + n], rt_s.at[2 + n], rt_r.at[2 + n], at_z(2 * (2 * n - 1))) for n in (0, 1)]

    def both(d):
        n = POS[d] if POS[d] < 4 else POS[d] - 4
        return GT[n] + CT[n].astype(F32)

    pair(0, 2)
    ST[0:4] = text_grad(1).astype(BF)
    ct(0).start()
    GT[0:4] = text_grad(0)
    pair(2, 2)
    ct(0).wait_recv()
    S2[4] = both(4).astype(BF)
    half_t[0].start()
    half_t[1].start()
    S2[2] = both(3).astype(BF)
    relay_t[3].start()
    S2[3] = both(5).astype(BF)
    relay_t[5].start()
    ST[4:8] = text_grad(3).astype(BF)
    ct(1).start()

    def r1(d):
        return push(SI.at[d, 1:4, pl.ds(0, H)], R1.at[d, 1:4], r1_s.at[d], r1_r.at[d], at_y(-d))

    def r2(d):
        return push(SI.at[1:4, d, pl.ds(H, H)], R2.at[d, 1:4], r2_s.at[d], r2_r.at[d], at_x(-d))

    def e1(d):
        return push(SI.at[d, 0, pl.ds(0, H)], R1.at[d, 0], e1_s.at[d], e1_r.at[d], at_y(-d))

    def e2(d):
        return push(SI.at[0, d, pl.ds(H, H)], R2.at[d, 0], e2_s.at[d], e2_r.at[d], at_x(-d))

    SI[...] = dot(PW[...], HT[...]).astype(BF).reshape(4, 4, R, W)
    for d in (2, 1, 3):
        r1(d).start()
        r2(d).start()
    for d in (2, 1, 3):
        e1(d).start()
        e2(d).start()

    GT[4:8] = text_grad(2)
    ct(1).wait_recv()
    S2[0] = both(1).astype(BF)
    near_t[1].start()
    S2[1] = both(7).astype(BF)
    near_t[7].start()

    for n, (d_near, d_far) in enumerate(((2, 3), (6, 5))):
        relay_t[d_far].wait_recv()
        half_t[n].wait_recv()
        m = both(d_near) + RA[n].astype(F32)
        extra = RB[n].astype(F32)
        rows, rest = (slice(0, H), slice(H, R)) if n == 0 else (slice(H, R), slice(0, H))
        RM[n, rows] = (m[rows] + extra).astype(BF)
        RM[n, rest] = m[rest].astype(BF)
        sum_t[n].start()

    def flip(j):
        lanes = pl.ds(pl.multiple_of(j * Q, Q), Q)
        XIT[lanes] = XI[:, :, :, lanes].reshape(B, Q).T
        XTT[lanes] = XT[:, :, lanes].reshape(B, Q).T

    each(0, NB, flip)

    def f1(d):
        return push(N1.at[d], F1.at[d], f1_s.at[d], f1_r.at[d], at_x(-d))

    def f2(d):
        return push(N2.at[d], F2.at[d], f2_s.at[d], f2_r.at[d], at_y(-d))

    arrived(r1(d) for d in (1, 3, 2))

    def sum1(d):
        N1[d] = (SI[0, d, 0:H].astype(F32) + R1[1, d].astype(F32) + R1[2, d].astype(F32) + R1[3, d].astype(F32)).astype(BF)

    def sum2(d):
        N2[d] = (SI[d, 0, H:R].astype(F32) + R2[1, d].astype(F32) + R2[2, d].astype(F32) + R2[3, d].astype(F32)).astype(BF)

    for d in (2, 1, 3):
        sum1(d)
        f1(d).start()
    arrived(r2(d) for d in (1, 3, 2))
    for d in (2, 1, 3):
        sum2(d)
        f2(d).start()

    def unembed(g, D, L, blocks):
        d = D[...]
        half = ((g - d * jnp.sum(d * g, axis=1, keepdims=True)) / L[...]).astype(BF)
        for j in range(NB):
            blocks[j] = half[:, j * Q : (j + 1) * Q]
        return half

    arrived((near_t[1], near_t[7], sum_t[0], sum_t[1]))
    g = both(0)
    for n in range(4):
        g = g + RT[n].astype(F32)
    half_text = unembed(g, DT, LT, TB)
    mine = jnp.where(k == 0, z, 8)

    def pt(s):
        zz = rem(z + s % 8, 8)
        kk = rem(k + s // 8, 2)
        slot = POS[s % 8] + 4 * (s // 8)
        return push(TB.at[jnp.where(kk == 0, zz, 8)], PT.at[slot], pt_s.at[s], pt_r.at[s], device(zz, y, x, kk))

    for s in (12, 11, 13, 4, 3, 5, 10, 14, 2, 6, 9, 15, 1, 7, 8):
        pt(s).start()
    PT[OWN] = TB[mine]

    arrived(e1(d) for d in (1, 3, 2))
    sum1(0)
    arrived(e2(d) for d in (1, 3, 2))
    sum2(0)
    arrived(f1(d) for d in (1, 3, 2))
    arrived(f2(d) for d in (1, 3, 2))
    g1 = N1[0].astype(F32)
    g2 = N2[0].astype(F32)
    for d in (1, 2, 3):
        g1 = g1 + F1[d].astype(F32)
        g2 = g2 + F2[d].astype(F32)
    half_image = unembed(jnp.concatenate([g1, g2], axis=0), DI, LI, GB)

    def plane_index(i):
        return rem(y + div(i, 4), 4) * 4 + rem(x + rem(i, 4), 4)

    def pi(i, block=None):
        block = plane_index(i) if block is None else block
        to = device(z, rem(y + div(i, 4), 4), rem(x + rem(i, 4), 4), k)
        return push(GB.at[block], PI.at[i], pi_s.at[i], pi_r.at[i], to)

    def pi_send(i):
        @pl.when(plane_index(i) < NB)
        def _():
            pi(i).start()

    each(1, 16, pi_send)
    sums_image = p0 < NB

    for s in range(1, 16):
        pt(s).wait_recv()
    PART[...] = dot(XTT[...], PT[...].reshape(B, Q))
    m, h = 2 * y + rem(x, 2), div(x, 2)
    zt = rem(m + 8 - z, 8)
    sums_text = (k == 0) | (m == z)

    def ut_place(u):
        return jnp.where(k == 0, rem(div(u, 2) + z, 8), z)

    def ut(u):
        at = ut_place(u)
        to = device(z, div(at, 2), 2 * rem(u, 2) + rem(at, 2), k)
        return push(VB.at[u], UT.at[p0], ut_s.at[u], ut_r.at[p0], to)

    def ut_here(u):
        return (ut_place(u) == m) & (rem(u, 2) == h)

    def ut_used(u):
        return (k == 0) | (div(u, 2) == z)

    def ut_send(i):
        u = rem(i + 2 * zt + 6, 16)

        @pl.when(ut_used(u))
        def _():
            VB[u, 0:U] = PART[pl.ds(pl.multiple_of(u * U, 8), U)].astype(BF)

            @pl.when(ut_here(u))
            def _():
                UT[p0] = VB[u]

            @pl.when(jnp.logical_not(ut_here(u)))
            def _():
                ut(u).start()

    each(0, 16, ut_send)

    def cb():
        return push(SB, CB, cb_s.at[0], cb_r.at[0], sib)

    def ui(d):
        return push(UB.at[d], UI.at[d], ui_s.at[d], ui_r.at[d], device(rem(z + d, 8), y, x, k))

    def head_rows(zz, h):
        return pl.ds(pl.multiple_of(zz * (2 * U) + h * U, 8), U)

    @pl.when(sums_image)
    def _():
        PI[0] = GB[p0]
        each(1, 16, lambda i: pi(i, 0).wait_recv())
        PARI[...] = dot(XIT[...], PI[...].reshape(B, Q))

        def give(d):
            SB[d, 0:U] = PARI[head_rows(rem(z + d, 8), 1 - k)].astype(BF)

        each(0, 8, give)
        cb().start()

    out[R : 2 * R] = dot_nt(half_text, WT[...])

    @pl.when(sums_image)
    def _():
        cb().wait_recv()

        def pass_on(i):
            d = rem(i + 4, 8)
            UB[d, 0:U] = (PARI[head_rows(rem(z + d, 8), k)] + CB[d, 0:U].astype(F32)).astype(BF)

            @pl.when(d > 0)
            def _():
                ui(d).start()

        each(0, 8, pass_on)

    block = jnp.where(k == 0, z, 8)
    zd = jnp.where(k == 0, zt, z)

    def ft(t):
        to = device(zd, rem(y + 2 + div(t, 2), 4), 2 * h + rem(t, 2), k)
        return push(CX, FT.at[block], ft_s.at[t], ft_r.at[block], to)

    def ft_here(t):
        return (zd == z) & (div(t, 2) == 2) & (rem(t, 2) == rem(x, 2))

    def fi(t):
        to = device(z, rem(y + 2 + div(t, 2), 4), k * 2 + rem(t, 2), k)
        return push(CI, FI.at[p0], fi_s.at[t], fi_r.at[p0], to)

    def fi_here(t):
        return (div(t, 2) == 2) & (k * 2 + rem(t, 2) == x)

    @pl.when(sums_text)
    def _():
        def add_text(q, acc):
            @pl.when(q != p0)
            def _():
                push(VB.at[0], UT.at[q], ut_s.at[0], ut_r.at[q], sib).wait_recv()

            return acc + UT[q, 0:U].astype(F32)

        CX[0:U] = lax.fori_loop(0, 16, add_text, jnp.zeros((U, Q), F32)).astype(BF)

        def send(t):
            @pl.when(ft_here(t))
            def _():
                FT[block] = CX[...]

            @pl.when(jnp.logical_not(ft_here(t)))
            def _():
                ft(t).start()

        each(0, 8, send)

    out[0:R] = dot_nt(half_image, WI[...])

    for copy in (*z_near.values(), *z_far.values(), *near_t.values(), *relay_t.values(), *half_t, *sum_t):
        copy.wait_send()
    for n in POS.values():
        ac(n).wait_send()
    for copy in (ax, ay, a1, a2, r1, r2, e1, e2, f1, f2):
        for d in (1, 2, 3):
            copy(d).wait_send()
    ct(0).wait_send()
    ct(1).wait_send()
    for s in range(1, 16):
        pt(s).wait_send()

    def pi_sent(i):
        @pl.when(plane_index(i) < NB)
        def _():
            pi(i, 0).wait_send()

    each(1, 16, pi_sent)

    @pl.when(sums_image)
    def _():
        def add_image(d, acc):
            ui(d).wait_recv()
            return acc + UI[d, 0:U].astype(F32)

        CI[0:U] = lax.fori_loop(1, 8, add_image, UB[0, 0:U].astype(F32)).astype(BF)

        def send(t):
            @pl.when(fi_here(t))
            def _():
                FI[p0] = CI[...]

            @pl.when(jnp.logical_not(fi_here(t)))
            def _():
                fi(t).start()

        each(0, 8, send)

    def ft_on(j):
        return push(FT.at[j], FT.at[j], fp_s.at[j], ft_r.at[j], sib)

    def fi_on(j):
        return push(FI.at[j], FI.at[j], fo_s.at[j], fi_r.at[j], sib)

    def ft_wait(j):
        mine_j = ((k == 1) & (m == z)) if j == 8 else ((k == 0) & (z == j) & (zt == z))

        @pl.when(jnp.logical_not(mine_j))
        def _():
            push(CX, FT.at[j], ft_s.at[0], ft_r.at[j], sib).wait_recv()

    for j in range(NB):

        @pl.when(k == j // 8)
        def _():
            ft_wait(j)
            ft_on(j).start()

    @pl.when(k == h)
    def _():
        for j in range(NB):

            @pl.when(p0 != j)
            def _():
                push(CI, FI.at[j], fi_s.at[0], fi_r.at[j], sib).wait_recv()

            fi_on(j).start()

    for j in range(NB):

        @pl.when(k != j // 8)
        def _():
            push(CX, FT.at[j], ft_s.at[0], ft_r.at[j], sib).wait_recv()

        out[2 * R + U :, j * Q : (j + 1) * Q] = FT[j, 0:U].astype(F32)

    def ut_sent(u):
        @pl.when(ut_used(u) & jnp.logical_not(ut_here(u)))
        def _():
            push(VB.at[0], UT.at[0], ut_s.at[u], ut_r.at[0], sib).wait_send()

    each(0, 16, ut_sent)

    @pl.when(sums_image)
    def _():
        cb().wait_send()
        each(1, 8, lambda d: ui(d).wait_send())

    @pl.when(sums_text)
    def _():
        def sent(t):
            @pl.when(jnp.logical_not(ft_here(t)))
            def _():
                push(CX, FT.at[0], ft_s.at[t], ft_r.at[0], sib).wait_send()

        each(0, 8, sent)

    for j in range(NB):

        @pl.when(k != h)
        def _():
            push(CI, FI.at[j], fi_s.at[0], fi_r.at[j], sib).wait_recv()

        out[2 * R : 2 * R + U, j * Q : (j + 1) * Q] = FI[j, 0:U].astype(F32)

    @pl.when(sums_image)
    def _():
        def sent(t):
            @pl.when(jnp.logical_not(fi_here(t)))
            def _():
                push(CI, FI.at[0], fi_s.at[t], fi_r.at[0], sib).wait_send()

        each(0, 8, sent)

    for j in range(NB):

        @pl.when(k == j // 8)
        def _():
            ft_on(j).wait_send()

    @pl.when(k == h)
    def _():
        for j in range(NB):
            fi_on(j).wait_send()


def body(image_features, text_features, image_weight, text_weight, log_scale, bias):
    vmem = pl.BlockSpec(memory_space=pltpu.VMEM)
    hbm = pl.BlockSpec(memory_space=pltpu.HBM)
    v = pltpu.VMEM
    dma = pltpu.SemaphoreType.DMA
    results = pl.pallas_call(
        kernel,
        out_shape=jax.ShapeDtypeStruct((2 * R + 2 * U, W), F32),
        in_specs=[hbm, hbm, hbm, hbm, vmem, vmem],
        out_specs=vmem,
        scratch_shapes=[
            v((W, W), BF), v((W, W), BF), v((4, 4, R, W), BF), v((16, R, W), BF), v((B, W), BF), v((B, W), BF), v((B, B), BF),
            v((W, B), BF), v((W, B), BF),
            v((R, W), F32), v((R, 1), F32), v((R, W), F32), v((R, 1), F32),
            v((8, R, W), BF), v((8, R, W), BF), v((8, R, W), F32), v((5, R, W), BF),
            v((2, R, W), BF), v((2, H, W), BF), v((2, R, W), BF), v((4, R, W), BF),
            v((4, 4, R, W), BF), v((4, 4, H, W), BF), v((4, 4, H, W), BF), v((4, H, W), BF), v((4, H, W), BF), v((4, H, W), BF), v((4, H, W), BF),
            v((NB, R, Q), BF), v((16, R, Q), BF), v((NB, R, Q), BF), v((16, R, Q), BF), v((W, Q), F32), v((W, Q), F32),
            v((8, UP, Q), BF), v((8, UP, Q), BF), v((8, UP, Q), BF), v((8, UP, Q), BF), v((16, UP, Q), BF), v((16, UP, Q), BF),
            v((UP, Q), BF), v((UP, Q), BF), v((NB, UP, Q), BF), v((NB, UP, Q), BF),
            dma((4,)), dma((8,)), dma((8,)), dma((12,)), dma((12,)), *[dma((4,)) for _ in range(8)],
            dma((2,)), dma((2,)), dma((2,)), dma((2,)), dma((2,)), dma((2,)), dma((4,)), dma((4,)), *[dma((4,)) for _ in range(12)],
            dma((16,)), dma((16,)), dma((16,)), dma((16,)), dma((1,)), dma((1,)), dma((8,)), dma((8,)),
            dma((16,)), dma((16,)), dma((8,)), dma((NB,)), dma((8,)), dma((NB,)), dma((NB,)), dma((NB,)),
        ],
        compiler_params=pltpu.CompilerParams(
            collective_id=0, has_side_effects=True, vmem_limit_bytes=52 * 1024 * 1024
        ),
    )(
        pltpu.with_memory_space_constraint(image_features, pltpu.HBM), pltpu.with_memory_space_constraint(text_features, pltpu.HBM), image_weight, text_weight,
        log_scale.reshape(1, 1), bias.reshape(1, 1),
    )

    return results[:R], results[R : 2 * R], results[2 * R : 2 * R + U], results[2 * R + U :]


def solution(mesh):
    in_specs = (P(("row", "col"), None), P(("col", "row"), None), P(), P(), P(), P())
    out_specs = (P(("row", "col"), None), P(("col", "row"), None), P("row", None), P("row", None))
    return jax.shard_map(body, mesh=mesh, in_specs=in_specs, out_specs=out_specs, check_vma=False)
```

```python
import jax
import jax.numpy as jnp
from jax import lax
from jax.experimental import pallas as pl
from jax.experimental.pallas import tpu as pltpu
from jax.sharding import PartitionSpec as P

MESH = pl.DeviceIdType.MESH
BF = jnp.bfloat16
F32 = jnp.float32
W = 1152
R = 32
H = 16
B = 512
Q = 128
U = 72
UP = 80
NB = 9
POS = {6: 0, 3: 1, 5: 2, 4: 3, 0: 8, 1: 9, 7: 10, 2: 11}
OWN = POS[0]


def div(a, b):
    return a // b if isinstance(a, int) else lax.div(a, jnp.int32(b))


def rem(a, b):
    return a % b if isinstance(a, int) else lax.rem(a, jnp.int32(b))


def place():
    r, c = lax.axis_index("row"), lax.axis_index("col")
    return div(r, 2), div(c, 4), rem(r, 2) * 2 + div(rem(c, 4), 2), rem(c, 2)


def device(z, y, x, k):
    return (z * 2 + div(x, 2), y * 4 + rem(x, 2) * 2 + k)


def push(src, dst, send, recv, to):
    return pltpu.make_async_remote_copy(
        src_ref=src, dst_ref=dst, send_sem=send, recv_sem=recv, device_id=to, device_id_type=MESH
    )


def dot(a, b):
    return jnp.dot(a, b, preferred_element_type=F32)


def dot_nt(a, b):
    return lax.dot_general(a, b, (((1,), (1,)), ((), ())), preferred_element_type=F32)


def dot_tn(a, b):
    return lax.dot_general(a, b, (((0,), (0,)), ((), ())), preferred_element_type=F32)


def each(lo, hi, fn):
    def step(i, carry):
        fn(i)
        return carry

    lax.fori_loop(lo, hi, step, 0)


def kernel(
    xi, xt, wi_hbm, wt_hbm, ls, bs,
    out,
    WI, WT, XI, XT, HI, HT, PW, XIT, XTT,
    DI, LI, DT, LT,
    ST, CT, GT, S2, RA, RB, RM, RT, SI, R1, R2, N1, N2, F1, F2,
    GB, PI, TB, PT, PARI, PART, SB, CB, UB, UI, VB, UT, CI, CX, FI, FT,
    lsem, at_s, at_r, ac_s, ac_r, ax_s, ax_r, ay_s, ay_r, a1_s, a1_r, a2_s, a2_r,
    ct_s, ct_r, ra_s, ra_r, rb_s, rb_r, rt_s, rt_r, r1_s, r1_r, r2_s, r2_r, e1_s, e1_r, e2_s, e2_r, f1_s, f1_r, f2_s, f2_r,
    pi_s, pi_r, pt_s, pt_r, cb_s, cb_r, ui_s, ui_r, ut_s, ut_r, fi_s, fi_r, ft_s, ft_r, fo_s, fp_s,
):
    z, y, x, k = place()
    p0 = y * 4 + x
    sib = device(z, y, x, 1 - k)

    def at_z(d):
        return device(rem(z + d + 8, 8), y, x, k)

    def at_y(d):
        return device(z, rem(y + d + 4, 4), x, k)

    def at_x(d):
        return device(z, y, rem(x + d + 4, 4), k)

    loads = [
        pltpu.make_async_copy(src, dst, lsem.at[n])
        for n, (src, dst) in enumerate(((xt, XT.at[OWN]), (xi, XI.at[0, 0]), (wt_hbm, WT), (wi_hbm, WI)))
    ]
    bar = pltpu.get_barrier_semaphore()
    near = [at_z(2), at_z(-2), at_x(2), at_y(2)] + [at(d) for at in (at_z, at_x, at_y) for d in (1, -1)] + [sib]
    for to in near:
        pl.semaphore_signal(bar, inc=1, device_id=to, device_id_type=MESH)
    for load in loads:
        load.start()

    pad = jnp.zeros((8, UP - U, Q), BF)
    for buf in (SB, UB, VB.at[0:8], VB.at[8:16]):
        buf[:, U:UP] = pad
    CI[U:UP] = pad[0]
    CX[U:UP] = pad[0]

    loads[0].wait()
    loads[1].wait()
    pl.semaphore_wait(bar, len(near))

    def tz(d, d_to, n, rows=None):
        src, dst = XT.at[POS[d % 8]], XT.at[POS[(d + d_to) % 8]]
        if rows is not None:
            src, dst = src.at[pl.ds(rows, H)], dst.at[pl.ds(rows, H)]
        return push(src, dst, at_s.at[n], at_r.at[n], at_z(d_to))

    z_near = {1: tz(0, 1, 0), 7: tz(0, -1, 1), 2: tz(0, 2, 2), 6: tz(0, -2, 3)}
    z_far = {3: tz(2, 1, 4), 5: tz(-2, -1, 5), 4: tz(2, 2, 6, 0), 12: tz(-2, -2, 7, H)}

    def ac(s):
        return push(XT.at[s], XT.at[s + 4], ac_s.at[s], ac_r.at[s], sib)

    def ax(d):
        return push(XI.at[0, 0], XI.at[0, d], ax_s.at[d], ax_r.at[d], at_x(d))

    def ay(d):
        return push(XI.at[0, 0], XI.at[d, 0], ay_s.at[d], ay_r.at[d], at_y(d))

    def a1(d):
        rows = pl.ds(0, H)
        return push(XI.at[0, 1:4, rows], XI.at[d, 1:4, rows], a1_s.at[d], a1_r.at[d], at_y(d))

    def a2(d):
        rows = pl.ds(H, H)
        return push(XI.at[1:4, 0, rows], XI.at[1:4, d, rows], a2_s.at[d], a2_r.at[d], at_x(d))

    z_near[2].start()
    z_near[6].start()
    for d in (2, 1, 3):
        ax(d).start()
        ay(d).start()
    z_near[1].start()
    z_near[7].start()
    ac(OWN).start()

    def project(x_in, n, WW, HH, c):
        p = dot(x_in.reshape(n * Q, W), WW[...])
        length = jnp.sqrt(jnp.sum(p * p, axis=1, keepdims=True) + 1e-06)
        p = p * (1.0 / length)
        HH[c * Q : (c + n) * Q] = p.astype(BF)
        return p, length

    def arrived(copies):
        for copy in copies:
            copy.wait_recv()

    z_near[2].wait_recv()
    z_far[4].start()
    z_far[3].start()
    ac(POS[2]).start()
    z_near[6].wait_recv()
    z_far[12].start()
    z_far[5].start()
    arrived(ax(d) for d in (1, 3, 2))
    for d in (2, 1, 3):
        a1(d).start()
    arrived(ay(d) for d in (1, 3, 2))
    for d in (2, 1, 3):
        a2(d).start()
    ac(POS[6]).start()
    for d in (1, 7):
        z_near[d].wait_recv()
        ac(POS[d]).start()

    loads[2].wait()
    p, length = project(XT[8:12], 1, WT, HT, 2)
    DT[...] = p[:R]
    LT[...] = length[:R]
    loads[3].wait()
    p, length = project(XI[0], 1, WI, HI, 0)
    DI[...] = p[:R]
    LI[...] = length[:R]

    arrived([z_far[3]])
    ac(POS[3]).start()
    arrived([z_far[5]])
    ac(POS[5]).start()
    arrived([z_far[4], z_far[12]])
    ac(POS[4]).start()
    arrived(ac(s) for s in (8, 9, 10, 11))
    project(XT[12:16], 1, WT, HT, 3)
    arrived(ac(s) for s in range(4))
    project(XT[0:8], 2, WT, HT, 0)
    arrived(a(d) for a in (a1, a2) for d in (1, 3, 2))
    project(XI[1:4], 3, WI, HI, 1)

    factor = jnp.exp(ls[...])
    bias = bs[...]
    col = lax.broadcasted_iota(jnp.int32, (1, B), 1)
    cs = col >> 5
    cd = jnp.zeros_like(cs)
    for d, n in POS.items():
        cd = jnp.where((cs & 11) == n, d, cd)
    cz = (z - cd) & 7
    ck = k ^ ((cs >> 2) & 1)
    tid = (y * 4 + rem(x, 2) * 2 + ck) * B + (cz * 2 + div(x, 2)) * R + (col & 31)
    row = lax.broadcasted_iota(jnp.int32, (B, 1), 0)
    rs = row >> 5
    ry = (y - (rs >> 2)) & 3
    rx = (x - (rs & 3)) & 3
    iid = (z * 2 + (rx >> 1)) * B + (ry * 4 + ((rx & 1) << 1) + k) * R + (row & 31)

    def pair(c, n):
        cols = slice(c * Q, (c + n) * Q)
        logits = factor * dot_nt(HI[...], HT[cols]) + bias
        same = iid == tid[:, cols]
        signed = jnp.where(same, -logits, logits)
        weight = factor / (1.0 + jnp.exp(-signed))
        PW[:, cols] = jnp.where(same, -weight, weight).astype(BF)

    def text_grad(c):
        return dot_tn(PW[:, c * Q : (c + 1) * Q], HI[...]).reshape(4, R, W)

    def ct(c):
        half = pl.ds(c * 4, 4)
        return push(ST.at[half], CT.at[half], ct_s.at[c], ct_r.at[c], sib)

    near_t = {1: push(S2.at[0], RT.at[0], rt_s.at[0], rt_r.at[0], at_z(-1)),
              7: push(S2.at[1], RT.at[1], rt_s.at[1], rt_r.at[1], at_z(1))}
    relay_t = {3: push(S2.at[2], RA.at[0], ra_s.at[0], ra_r.at[0], at_z(-1)),
               5: push(S2.at[3], RA.at[1], ra_s.at[1], ra_r.at[1], at_z(1))}
    half_t = [push(S2.at[4, pl.ds(n * H, H)], RB.at[n], rb_s.at[n], rb_r.at[n], at_z(2 * (2 * n - 1))) for n in (0, 1)]
    sum_t = [push(RM.at[n], RT.at[2 + n], rt_s.at[2 + n], rt_r.at[2 + n], at_z(2 * (2 * n - 1))) for n in (0, 1)]

    def both(d):
        n = POS[d] if POS[d] < 4 else POS[d] - 4
        return GT[n] + CT[n].astype(F32)

    pair(0, 2)
    ST[0:4] = text_grad(1).astype(BF)
    ct(0).start()
    GT[0:4] = text_grad(0)
    pair(2, 2)
    ct(0).wait_recv()
    S2[4] = both(4).astype(BF)
    half_t[0].start()
    half_t[1].start()
    S2[2] = both(3).astype(BF)
    relay_t[3].start()
    S2[3] = both(5).astype(BF)
    relay_t[5].start()
    ST[4:8] = text_grad(3).astype(BF)
    ct(1).start()

    def r1(d):
        return push(SI.at[d, 1:4, pl.ds(0, H)], R1.at[d, 1:4], r1_s.at[d], r1_r.at[d], at_y(-d))

    def r2(d):
        return push(SI.at[1:4, d, pl.ds(H, H)], R2.at[d, 1:4], r2_s.at[d], r2_r.at[d], at_x(-d))

    def e1(d):
        return push(SI.at[d, 0, pl.ds(0, H)], R1.at[d, 0], e1_s.at[d], e1_r.at[d], at_y(-d))

    def e2(d):
        return push(SI.at[0, d, pl.ds(H, H)], R2.at[d, 0], e2_s.at[d], e2_r.at[d], at_x(-d))

    SI[...] = dot(PW[...], HT[...]).astype(BF).reshape(4, 4, R, W)
    for d in (2, 1, 3):
        r1(d).start()
        r2(d).start()
    for d in (2, 1, 3):
        e1(d).start()
        e2(d).start()

    GT[4:8] = text_grad(2)
    ct(1).wait_recv()
    S2[0] = both(1).astype(BF)
    near_t[1].start()
    S2[1] = both(7).astype(BF)
    near_t[7].start()

    for n, (d_near, d_far) in enumerate(((2, 3), (6, 5))):
        relay_t[d_far].wait_recv()
        half_t[n].wait_recv()
        m = both(d_near) + RA[n].astype(F32)
        extra = RB[n].astype(F32)
        rows, rest = (slice(0, H), slice(H, R)) if n == 0 else (slice(H, R), slice(0, H))
        RM[n, rows] = (m[rows] + extra).astype(BF)
        RM[n, rest] = m[rest].astype(BF)
        sum_t[n].start()

    def flip(j):
        lanes = pl.ds(pl.multiple_of(j * Q, Q), Q)
        XIT[lanes] = XI[:, :, :, lanes].reshape(B, Q).T
        XTT[lanes] = XT[:, :, lanes].reshape(B, Q).T

    each(0, NB, flip)

    def f1(d):
        return push(N1.at[d], F1.at[d], f1_s.at[d], f1_r.at[d], at_x(-d))

    def f2(d):
        return push(N2.at[d], F2.at[d], f2_s.at[d], f2_r.at[d], at_y(-d))

    arrived(r1(d) for d in (1, 3, 2))

    def sum1(d):
        N1[d] = (SI[0, d, 0:H].astype(F32) + R1[1, d].astype(F32) + R1[2, d].astype(F32) + R1[3, d].astype(F32)).astype(BF)

    def sum2(d):
        N2[d] = (SI[d, 0, H:R].astype(F32) + R2[1, d].astype(F32) + R2[2, d].astype(F32) + R2[3, d].astype(F32)).astype(BF)

    for d in (2, 1, 3):
        sum1(d)
        f1(d).start()
    arrived(r2(d) for d in (1, 3, 2))
    for d in (2, 1, 3):
        sum2(d)
        f2(d).start()

    def unembed(g, D, L, blocks):
        d = D[...]
        half = ((g - d * jnp.sum(d * g, axis=1, keepdims=True)) / L[...]).astype(BF)
        for j in range(NB):
            blocks[j] = half[:, j * Q : (j + 1) * Q]
        return half

    arrived((near_t[1], near_t[7], sum_t[0], sum_t[1]))
    g = both(0)
    for n in range(4):
        g = g + RT[n].astype(F32)
    half_text = unembed(g, DT, LT, TB)
    mine = jnp.where(k == 0, z, 8)

    def pt(s):
        zz = rem(z + s % 8, 8)
        kk = rem(k + s // 8, 2)
        slot = POS[s % 8] + 4 * (s // 8)
        return push(TB.at[jnp.where(kk == 0, zz, 8)], PT.at[slot], pt_s.at[s], pt_r.at[s], device(zz, y, x, kk))

    for s in (12, 11, 13, 4, 3, 5, 10, 14, 2, 6, 9, 15, 1, 7, 8):
        pt(s).start()
    PT[OWN] = TB[mine]

    arrived(e1(d) for d in (1, 3, 2))
    sum1(0)
    arrived(e2(d) for d in (1, 3, 2))
    sum2(0)
    arrived(f1(d) for d in (1, 3, 2))
    arrived(f2(d) for d in (1, 3, 2))
    g1 = N1[0].astype(F32)
    g2 = N2[0].astype(F32)
    for d in (1, 2, 3):
        g1 = g1 + F1[d].astype(F32)
        g2 = g2 + F2[d].astype(F32)
    half_image = unembed(jnp.concatenate([g1, g2], axis=0), DI, LI, GB)

    def plane_index(i):
        return rem(y + div(i, 4), 4) * 4 + rem(x + rem(i, 4), 4)

    def pi(i, block=None):
        block = plane_index(i) if block is None else block
        to = device(z, rem(y + div(i, 4), 4), rem(x + rem(i, 4), 4), k)
        return push(GB.at[block], PI.at[i], pi_s.at[i], pi_r.at[i], to)

    def pi_send(i):
        @pl.when(plane_index(i) < NB)
        def _():
            pi(i).start()

    each(1, 16, pi_send)
    sums_image = p0 < NB

    for s in range(1, 16):
        pt(s).wait_recv()
    PART[...] = dot(XTT[...], PT[...].reshape(B, Q))
    m, h = 2 * y + rem(x, 2), div(x, 2)
    zt = rem(m + 8 - z, 8)
    sums_text = (k == 0) | (m == z)

    def ut_place(u):
        return jnp.where(k == 0, rem(div(u, 2) + z, 8), z)

    def ut(u):
        at = ut_place(u)
        to = device(z, div(at, 2), 2 * rem(u, 2) + rem(at, 2), k)
        return push(VB.at[u], UT.at[p0], ut_s.at[u], ut_r.at[p0], to)

    def ut_here(u):
        return (ut_place(u) == m) & (rem(u, 2) == h)

    def ut_used(u):
        return (k == 0) | (div(u, 2) == z)

    def ut_send(i):
        u = rem(i + 2 * zt + 6, 16)

        @pl.when(ut_used(u))
        def _():
            VB[u, 0:U] = PART[pl.ds(pl.multiple_of(u * U, 8), U)].astype(BF)

            @pl.when(ut_here(u))
            def _():
                UT[p0] = VB[u]

            @pl.when(jnp.logical_not(ut_here(u)))
            def _():
                ut(u).start()

    each(0, 16, ut_send)

    def cb():
        return push(SB, CB, cb_s.at[0], cb_r.at[0], sib)

    def ui(d):
        return push(UB.at[d], UI.at[d], ui_s.at[d], ui_r.at[d], device(rem(z + d, 8), y, x, k))

    def head_rows(zz, h):
        return pl.ds(pl.multiple_of(zz * (2 * U) + h * U, 8), U)

    @pl.when(sums_image)
    def _():
        PI[0] = GB[p0]
        each(1, 16, lambda i: pi(i, 0).wait_recv())
        PARI[...] = dot(XIT[...], PI[...].reshape(B, Q))

        def give(d):
            SB[d, 0:U] = PARI[head_rows(rem(z + d, 8), 1 - k)].astype(BF)

        each(0, 8, give)
        cb().start()

    out[R : 2 * R] = dot_nt(half_text, WT[...])

    @pl.when(sums_image)
    def _():
        cb().wait_recv()

        def pass_on(i):
            d = rem(i + 4, 8)
            UB[d, 0:U] = (PARI[head_rows(rem(z + d, 8), k)] + CB[d, 0:U].astype(F32)).astype(BF)

            @pl.when(d > 0)
            def _():
                ui(d).start()

        each(0, 8, pass_on)

    block = jnp.where(k == 0, z, 8)
    zd = jnp.where(k == 0, zt, z)

    def ft(t):
        to = device(zd, rem(y + 2 + div(t, 2), 4), 2 * h + rem(t, 2), k)
        return push(CX, FT.at[block], ft_s.at[t], ft_r.at[block], to)

    def ft_here(t):
        return (zd == z) & (div(t, 2) == 2) & (rem(t, 2) == rem(x, 2))

    def fi(t):
        to = device(z, rem(y + 2 + div(t, 2), 4), k * 2 + rem(t, 2), k)
        return push(CI, FI.at[p0], fi_s.at[t], fi_r.at[p0], to)

    def fi_here(t):
        return (div(t, 2) == 2) & (k * 2 + rem(t, 2) == x)

    @pl.when(sums_text)
    def _():
        def add_text(q, acc):
            @pl.when(q != p0)
            def _():
                push(VB.at[0], UT.at[q], ut_s.at[0], ut_r.at[q], sib).wait_recv()

            return acc + UT[q, 0:U].astype(F32)

        CX[0:U] = lax.fori_loop(0, 16, add_text, jnp.zeros((U, Q), F32)).astype(BF)

        def send(t):
            @pl.when(ft_here(t))
            def _():
                FT[block] = CX[...]

            @pl.when(jnp.logical_not(ft_here(t)))
            def _():
                ft(t).start()

        each(0, 8, send)

    out[0:R] = dot_nt(half_image, WI[...])

    for copy in (*z_near.values(), *z_far.values(), *near_t.values(), *relay_t.values(), *half_t, *sum_t):
        copy.wait_send()
    for n in POS.values():
        ac(n).wait_send()
    for copy in (ax, ay, a1, a2, r1, r2, e1, e2, f1, f2):
        for d in (1, 2, 3):
            copy(d).wait_send()
    ct(0).wait_send()
    ct(1).wait_send()
    for s in range(1, 16):
        pt(s).wait_send()

    def pi_sent(i):
        @pl.when(plane_index(i) < NB)
        def _():
            pi(i, 0).wait_send()

    each(1, 16, pi_sent)

    @pl.when(sums_image)
    def _():
        def add_image(d, acc):
            ui(d).wait_recv()
            return acc + UI[d, 0:U].astype(F32)

        CI[0:U] = lax.fori_loop(1, 8, add_image, UB[0, 0:U].astype(F32)).astype(BF)

        def send(t):
            @pl.when(fi_here(t))
            def _():
                FI[p0] = CI[...]

            @pl.when(jnp.logical_not(fi_here(t)))
            def _():
                fi(t).start()

        each(0, 8, send)

    def ft_on(j):
        return push(FT.at[j], FT.at[j], fp_s.at[j], ft_r.at[j], sib)

    def fi_on(j):
        return push(FI.at[j], FI.at[j], fo_s.at[j], fi_r.at[j], sib)

    def ft_wait(j):
        mine_j = ((k == 1) & (m == z)) if j == 8 else ((k == 0) & (z == j) & (zt == z))

        @pl.when(jnp.logical_not(mine_j))
        def _():
            push(CX, FT.at[j], ft_s.at[0], ft_r.at[j], sib).wait_recv()

    for j in range(NB):

        @pl.when(k == j // 8)
        def _():
            ft_wait(j)
            ft_on(j).start()

    @pl.when(k == h)
    def _():
        for j in range(NB):

            @pl.when(p0 != j)
            def _():
                push(CI, FI.at[j], fi_s.at[0], fi_r.at[j], sib).wait_recv()

            fi_on(j).start()

    for j in range(NB):

        @pl.when(k != j // 8)
        def _():
            push(CX, FT.at[j], ft_s.at[0], ft_r.at[j], sib).wait_recv()

        out[2 * R + U :, j * Q : (j + 1) * Q] = FT[j, 0:U].astype(F32)

    def ut_sent(u):
        @pl.when(ut_used(u) & jnp.logical_not(ut_here(u)))
        def _():
            push(VB.at[0], UT.at[0], ut_s.at[u], ut_r.at[0], sib).wait_send()

    each(0, 16, ut_sent)

    @pl.when(sums_image)
    def _():
        cb().wait_send()
        each(1, 8, lambda d: ui(d).wait_send())

    @pl.when(sums_text)
    def _():
        def sent(t):
            @pl.when(jnp.logical_not(ft_here(t)))
            def _():
                push(CX, FT.at[0], ft_s.at[t], ft_r.at[0], sib).wait_send()

        each(0, 8, sent)

    for j in range(NB):

        @pl.when(k != h)
        def _():
            push(CI, FI.at[j], fi_s.at[0], fi_r.at[j], sib).wait_recv()

        out[2 * R : 2 * R + U, j * Q : (j + 1) * Q] = FI[j, 0:U].astype(F32)

    @pl.when(sums_image)
    def _():
        def sent(t):
            @pl.when(jnp.logical_not(fi_here(t)))
            def _():
                push(CI, FI.at[0], fi_s.at[t], fi_r.at[0], sib).wait_send()

        each(0, 8, sent)

    for j in range(NB):

        @pl.when(k == j // 8)
        def _():
            ft_on(j).wait_send()

    @pl.when(k == h)
    def _():
        for j in range(NB):
            fi_on(j).wait_send()


def body(image_features, text_features, image_weight, text_weight, log_scale, bias):
    vmem = pl.BlockSpec(memory_space=pltpu.VMEM)
    hbm = pl.BlockSpec(memory_space=pltpu.HBM)
    v = pltpu.VMEM
    dma = pltpu.SemaphoreType.DMA
    results = pl.pallas_call(
        kernel,
        out_shape=jax.ShapeDtypeStruct((2 * R + 2 * U, W), F32),
        in_specs=[hbm, hbm, hbm, hbm, vmem, vmem],
        out_specs=vmem,
        scratch_shapes=[
            v((W, W), BF), v((W, W), BF), v((4, 4, R, W), BF), v((16, R, W), BF), v((B, W), BF), v((B, W), BF), v((B, B), BF),
            v((W, B), BF), v((W, B), BF),
            v((R, W), F32), v((R, 1), F32), v((R, W), F32), v((R, 1), F32),
            v((8, R, W), BF), v((8, R, W), BF), v((8, R, W), F32), v((5, R, W), BF),
            v((2, R, W), BF), v((2, H, W), BF), v((2, R, W), BF), v((4, R, W), BF),
            v((4, 4, R, W), BF), v((4, 4, H, W), BF), v((4, 4, H, W), BF), v((4, H, W), BF), v((4, H, W), BF), v((4, H, W), BF), v((4, H, W), BF),
            v((NB, R, Q), BF), v((16, R, Q), BF), v((NB, R, Q), BF), v((16, R, Q), BF), v((W, Q), F32), v((W, Q), F32),
            v((8, UP, Q), BF), v((8, UP, Q), BF), v((8, UP, Q), BF), v((8, UP, Q), BF), v((16, UP, Q), BF), v((16, UP, Q), BF),
            v((UP, Q), BF), v((UP, Q), BF), v((NB, UP, Q), BF), v((NB, UP, Q), BF),
            dma((4,)), dma((8,)), dma((8,)), dma((12,)), dma((12,)), *[dma((4,)) for _ in range(8)],
            dma((2,)), dma((2,)), dma((2,)), dma((2,)), dma((2,)), dma((2,)), dma((4,)), dma((4,)), *[dma((4,)) for _ in range(12)],
            dma((16,)), dma((16,)), dma((16,)), dma((16,)), dma((1,)), dma((1,)), dma((8,)), dma((8,)),
            dma((16,)), dma((16,)), dma((8,)), dma((NB,)), dma((8,)), dma((NB,)), dma((NB,)), dma((NB,)),
        ],
        compiler_params=pltpu.CompilerParams(
            collective_id=0, has_side_effects=True, vmem_limit_bytes=52 * 1024 * 1024
        ),
    )(
        pltpu.with_memory_space_constraint(image_features, pltpu.HBM), pltpu.with_memory_space_constraint(text_features, pltpu.HBM), image_weight, text_weight,
        log_scale.reshape(1, 1), bias.reshape(1, 1),
    )

    return results[:R], results[R : 2 * R], results[2 * R : 2 * R + U], results[2 * R + U :]


def solution(mesh):
    in_specs = (P(("row", "col"), None), P(("col", "row"), None), P(), P(), P(), P())
    out_specs = (P(("row", "col"), None), P(("col", "row"), None), P("row", None), P("row", None))
    return jax.shard_map(body, mesh=mesh, in_specs=in_specs, out_specs=out_specs, check_vma=False)
```
